128 devices in a mesh: ctx: 8 (over z, core), ch: 16 (over x, y).
Axes of the slice: x: 4, y: 4, z: 4, core: 2. Of those that a mesh axis runs over, the one named last changes fastest.
Arguments:
- out_gate: bfloat16 [1024, 4096], P('ctx', 'ch'), may hold values from -6 to 6
- in_gate: bfloat16 [1024, 4096], P('ctx', 'ch'), may hold values from -6 to 6
- signal: bfloat16 [1024, 4096], P('ctx', 'ch'), may hold values from -6 to 6
- cotangent: bfloat16 [1024, 4096], P('ctx', 'ch'), may hold values from -6 to 6
- filters: float32 [1024, 256], P('ctx', 'ch'), may hold values from -0.1875 to 0.1875
- block_ids: int32 [16], P('ctx'), may hold values from 0 to 15, each once
Outputs:
- outer_grad: bfloat16 [1024, 4096], P('ctx', 'ch')
- inner_grad: bfloat16 [1024, 4096], P('ctx', 'ch')
- signal_grad: bfloat16 [1024, 4096], P('ctx', 'ch')
- filter_grad: float32 [1024, 256], P('ctx', 'ch')
The draws below stay inside these ranges and needn't reach their ends.
Inputs may be any that keep to these rules, and one draw needn't show every extreme that they name: block_ids is a permutation of the context blocks.
All inputs are finite; a program needn't handle non-finite values.
Results may differ from the reference program's by a relative error of at most 0.005.
Values may be sent and summed in bfloat16 or wider, within the bound.
A program may use at most 64 MiB of HBM per device.

```python
import jax
import jax.numpy as jnp
from jax import lax

C = 4096
FG = 256
B = 64
NB = 16
L = 1024


def block_scale(rng, shape, split, low, high):
    loudness = 1.0
    for dim, blocks in split:
        steps = jax.random.uniform(jax.random.fold_in(jax.random.fold_in(rng, 6), dim), (blocks,), jnp.float32, low / len(split), high / len(split))
        loudness = loudness * jnp.repeat(jnp.exp(steps), shape[dim] // blocks).reshape((-1,) + (1,) * (len(shape) - 1 - dim))
    return loudness


def gaussian(own_key, extent, spread, bound, split=(), kind=jnp.bfloat16):
    gain = block_scale(own_key, extent, split, -0.22, 0.18) if split else 1.0
    entries = jax.random.normal(own_key, extent, jnp.float32) * spread * gain
    return jnp.minimum(jnp.maximum(entries, -bound), bound).astype(kind)


def setup_inputs(seed: int = 0) -> dict:
    splits = jax.random.split(jax.random.key(seed), 7)
    out_gate = gaussian(splits[0], (L, C), 1.0, 6.0, ((0, 8), (1, 16)))
    in_gate = gaussian(splits[1], (L, C), 1.0, 6.0, ((0, 8), (1, 16)))
    signal = gaussian(splits[2], (L, C), 1.0, 6.0, ((0, 8), (1, 16)))
    cotangent = gaussian(splits[3], (L, C), 1.0, 6.0, ((0, 8), (1, 16)))
    filters = gaussian(splits[4], (L, FG), L ** -0.5, 0.1875, ((0, 8), (1, 16)), jnp.float32)
    block_ids = jax.random.permutation(splits[5], NB).astype(jnp.int32)
    return {"out_gate": out_gate, "in_gate": in_gate, "signal": signal, "cotangent": cotangent, "filters": filters, "block_ids": block_ids}


def causal_conv(kernel, source):
    length = 2 * kernel.shape[0]
    spec = jnp.fft.rfft(kernel, n=length, axis=0) * jnp.fft.rfft(source, n=length, axis=0)
    return jnp.fft.irfft(spec, n=length, axis=0)[:kernel.shape[0]]


def correlate(kernel, source):
    length = 2 * kernel.shape[0]
    spec = jnp.conj(jnp.fft.rfft(kernel, n=length, axis=0)) * jnp.fft.rfft(source, n=length, axis=0)
    return jnp.fft.irfft(spec, n=length, axis=0)[:kernel.shape[0]]


def reference(out_gate, in_gate, signal, cotangent, filters, block_ids):
    order = jnp.argsort(block_ids).astype(jnp.int32)

    def to_pos(array):
        return array.reshape(NB, B, -1)[order].reshape(NB * B, -1)

    def to_store(array):
        return array.reshape(NB, B, -1)[block_ids].reshape(NB * B, -1)

    outer = to_pos(out_gate).astype(jnp.float32)
    inner = to_pos(in_gate).astype(jnp.float32)
    values = to_pos(signal).astype(jnp.float32)
    upstream = to_pos(cotangent).astype(jnp.float32)
    wide = jnp.tile(filters, (1, C // FG))
    product = lax.optimization_barrier((inner * values).astype(jnp.bfloat16)).astype(jnp.float32)
    weighted = lax.optimization_barrier((upstream * outer).astype(jnp.bfloat16)).astype(jnp.float32)
    conv = causal_conv(wide, product)
    outer_grad = (upstream * conv).astype(jnp.bfloat16)
    back = correlate(wide, weighted)
    inner_grad = (back * values).astype(jnp.bfloat16)
    signal_grad = (back * inner).astype(jnp.bfloat16)
    per_channel = correlate(product, weighted)
    filter_grad = jnp.sum(per_channel.reshape(NB * B, C // FG, FG), axis=1)
    return to_store(outer_grad), to_store(inner_grad), to_store(signal_grad), filter_grad
```

```python
from functools import partial

import jax
import jax.numpy as jnp
from jax import lax
from jax.experimental import pallas as pl
from jax.experimental.pallas import tpu as pltpu
from jax.sharding import PartitionSpec as P

MESH = pl.DeviceIdType.MESH
BF16 = jnp.bfloat16
F32 = jnp.float32
HALF = 64
SPAN = 128


def iota(shape, dim):
    return lax.broadcasted_iota(jnp.int32, shape, dim)


def mm(left, right, dims=((1,), (0,))):
    return lax.dot_general(left, right, (dims, ((), ())), preferred_element_type=F32)


def wait_all(ref, count, sem):
    view = ref.at[pl.ds(0, count)]
    pltpu.make_async_copy(view, view, sem).wait()


def swap_matrix(outer, inner):
    size = outer * inner
    row = iota((size, size), 0)
    col = iota((size, size), 1)
    hit = (row // outer == col % inner) & (row % outer == col // inner)
    return jnp.where(hit, 1.0, 0.0).astype(BF16)


def toeplitz(taps, length):
    base = jnp.broadcast_to(taps, (8, length))
    row = iota((8, length), 0)
    for bit in (1, 2, 4):
        base = jnp.where((row & bit) != 0, pltpu.roll(base, bit, 1), base)
    rows = [base] + [pltpu.roll(base, 8 * k, 1) for k in range(1, SPAN // 8)]
    full = jnp.concatenate(rows, axis=0)
    keep = iota((SPAN, length), 1) >= iota((SPAN, length), 0)
    return jnp.where(keep, full, 0.0)


def diagonals(table, length):
    keep = iota((SPAN, length), 1) >= iota((SPAN, length), 0)
    table = jnp.where(keep, table, 0.0)
    total = table[:8]
    for k in range(1, SPAN // 8):
        total = total + pltpu.roll(table[8 * k : 8 * k + 8], length - 8 * k, 1)
    row = iota((8, length), 0)
    for bit in (1, 2, 4):
        total = jnp.where((row & bit) != 0, pltpu.roll(total, length - bit, 1), total)
    return jnp.sum(total, axis=0, keepdims=True)


def kernel(
    nz,
    nj,
    nf,
    ids_ref,
    og_ref,
    ig_ref,
    sg_ref,
    ct_ref,
    fl_ref,
    outer_ref,
    inner_ref,
    signal_ref,
    fgrad_ref,
    w_send,
    w_recv,
    b_send,
    b_recv,
    a_send,
    a_recv,
    a2_send,
    a2_recv,
    b2_send,
    b2_recv,
    g_send,
    g_recv,
    send_sems,
    recv_sems,
):
    zi = lax.axis_index("ctx")
    ji = lax.axis_index("ch")
    nr = nf // nz
    rows = nz * nj
    length = nz * SPAN

    def ctx_peer(step):
        return lax.rem(zi + step, nz)

    def ch_peer(step):
        return lax.rem(ji + step, nj)

    barrier = pltpu.get_barrier_semaphore()
    for step in range(1, nz):
        pl.semaphore_signal(barrier, inc=1, device_id=(ctx_peer(step), ji), device_id_type=MESH)
    for step in range(1, nj):
        pl.semaphore_signal(barrier, inc=1, device_id=(zi, ch_peer(step)), device_id_type=MESH)

    def over_ctx(send, recv, k):
        for step in range(1, nz):
            q = ctx_peer(step)
            pltpu.make_async_remote_copy(
                send.at[q], recv.at[zi], send_sems.at[k], recv_sems.at[k], (q, ji), MESH
            ).start()
        recv[zi] = send[zi]

    def over_ch(send, recv, k):
        for step in range(1, nj):
            j = ch_peer(step)
            pltpu.make_async_remote_copy(
                send.at[j], recv.at[ji], send_sems.at[k], recv_sems.at[k], (zi, j), MESH
            ).start()
        recv[ji] = send[ji]

    product = ig_ref[...].astype(F32) * sg_ref[...].astype(F32)
    weighted = ct_ref[...].astype(F32) * og_ref[...].astype(F32)
    b_send[:, 0] = product.T.astype(BF16).reshape(nj, nf, SPAN)
    b_send[:, 1] = weighted.T.astype(BF16).reshape(nj, nf, SPAN)

    taps = fl_ref[...].T
    row8 = iota((8, SPAN), 0)
    id_lo = ids_ref[0].astype(F32)
    id_hi = ids_ref[1].astype(F32)
    tail = jnp.where(row8 == nr, id_lo, jnp.where(row8 == nr + 1, id_hi, 0.0))
    for q in range(nz):
        w_send[q] = tail
        w_send[q, 0:nr] = taps[q * nr : (q + 1) * nr]

    pl.semaphore_wait(barrier, nz + nj - 2)
    over_ch(b_send, b_recv, 0)
    over_ctx(w_send, w_recv, 1)

    swap = swap_matrix(nj, nf)
    wait_all(w_recv, nz - 1, recv_sems.at[1])
    bands = []
    for r in range(nr):
        line = jnp.concatenate([w_recv[z, r : r + 1] for z in range(nz)], axis=1)
        bands.append(toeplitz(line, length).astype(BF16))
    row = iota((rows, rows), 0)
    col = iota((rows, rows), 1)
    same_c = (row % nj) == (col % nj)
    by_row, by_col = [], []
    for h in range(2):
        lines = [w_recv[z, nr + h : nr + h + 1] for z in range(nz)]
        by_row.append(
            jnp.concatenate([jnp.broadcast_to(v[:, :rows], (nj, rows)) for v in lines], axis=0)
        )
        lane = iota((1, rows), 1) // nj
        mixed = jnp.zeros((1, rows), F32)
        for z in range(nz):
            mixed = jnp.where(lane == z, lines[z][:, :rows], mixed)
        by_col.append(jnp.broadcast_to(mixed, (rows, rows)))

    def one_hot(hit):
        return jnp.where(hit & same_c, 1.0, 0.0).astype(BF16)

    to_pos, to_store = [], []
    for kind in range(2):
        to_pos.append(
            [one_hot(by_col[h] == (2 * (row // nj) + (h ^ kind)).astype(F32)) for h in range(2)]
        )
        to_store.append(
            [one_hot(by_row[h ^ kind] == (2 * (col // nj) + h).astype(F32)) for h in range(2)]
        )

    def stack(parts):
        return jnp.concatenate([jnp.concatenate(part, axis=1) for part in parts], axis=0)

    to_pos = stack(to_pos)
    to_store = stack(to_store)

    def reorder(matrix, values):
        low = (iota(values.shape, 1) % SPAN) < HALF
        zero = jnp.zeros_like(values)
        halves = jnp.concatenate(
            [jnp.where(low, values, zero), jnp.where(low, zero, values)], axis=0
        )
        moved = mm(matrix, halves)
        parts = []
        for k in range(values.shape[1] // SPAN):
            lanes = slice(k * SPAN, (k + 1) * SPAN)
            parts.append(moved[:rows, lanes] + pltpu.roll(moved[rows:, lanes], HALF, 1))
        return parts

    wait_all(b_recv, nj - 1, recv_sems.at[0])
    arrived = jnp.concatenate(
        [b_recv[:, k].reshape(nj * nf, SPAN) for k in range(2)], axis=1
    )
    turned = mm(swap, arrived).astype(BF16)
    for k in range(2):
        a_send[:, k] = turned[:, k * SPAN : (k + 1) * SPAN].reshape(nz, nr, nj, SPAN)
    over_ctx(a_send, a_recv, 2)
    wait_all(a_recv, nz - 1, recv_sems.at[2])
    stored = jnp.concatenate(
        [a_recv[:, k, r].reshape(rows, SPAN) for k in range(2) for r in range(nr)], axis=1
    )
    ordered = reorder(to_pos, stored)

    results = [None] * (2 * nr)
    for r in range(nr):
        p = ordered[r].astype(BF16)
        g = ordered[nr + r].astype(BF16)
        band = bands[r]
        ahead = mm(p, band)
        stacked = jnp.concatenate(
            [band[:, d * SPAN : (d + 1) * SPAN] for d in range(nz)], axis=0
        )
        behind = mm(g, stacked, ((1,), (1,)))
        conv, back = [], []
        for t in range(nz):
            conv.append(
                sum(
                    ahead[i * nj : (i + 1) * nj, (t - i) * SPAN : (t - i + 1) * SPAN]
                    for i in range(t + 1)
                )
            )
            back.append(
                sum(
                    behind[j * nj : (j + 1) * nj, (j - t) * SPAN : (j - t + 1) * SPAN]
                    for j in range(t, nz)
                )
            )
        results[r] = jnp.concatenate(conv, axis=0).astype(BF16)
        results[nr + r] = jnp.concatenate(back, axis=0).astype(BF16)

    restored = reorder(to_store, jnp.concatenate(results, axis=1))
    for k in range(2):
        for r in range(nr):
            a2_send[:, k, r] = restored[k * nr + r].astype(BF16).reshape(nz, nj, SPAN)
    over_ctx(a2_send, a2_recv, 3)

    sums = []
    for r in range(nr):
        p_turned = ordered[r].T.astype(BF16)
        g = ordered[nr + r].astype(BF16)
        shifted = [g] + [
            jnp.concatenate([g[d * nj :], jnp.zeros((d * nj, SPAN), BF16)], axis=0)
            for d in range(1, nz)
        ]
        sums.append(diagonals(mm(p_turned, jnp.concatenate(shifted, axis=1)), length))
    for z in range(nz):
        tile = jnp.zeros((8, SPAN), F32)
        for r in range(nr):
            tile = jnp.where(row8 == r, sums[r][:, z * SPAN : (z + 1) * SPAN], tile)
        g_send[z] = tile
    over_ctx(g_send, g_recv, 4)

    wait_all(a2_recv, nz - 1, recv_sems.at[3])
    came = jnp.concatenate(
        [a2_recv[:, k].reshape(nf * nj, SPAN) for k in range(2)], axis=1
    )
    back_turned = mm(swap.T if nj != nf else swap, came).astype(BF16)
    for k in range(2):
        b2_send[:, k] = back_turned[:, k * SPAN : (k + 1) * SPAN].reshape(nj, nf, SPAN)
    over_ch(b2_send, b2_recv, 5)

    wait_all(g_recv, nz - 1, recv_sems.at[4])
    grads = jnp.concatenate([g_recv[q, 0:nr] for q in range(nz)], axis=0)
    fgrad_ref[...] = grads.T

    wait_all(b2_recv, nj - 1, recv_sems.at[5])
    conv = b2_recv[:, 0].reshape(nj * nf, SPAN).astype(F32).T
    back = b2_recv[:, 1].reshape(nj * nf, SPAN).astype(F32).T
    outer_ref[...] = (ct_ref[...].astype(F32) * conv).astype(BF16)
    inner_ref[...] = (back * sg_ref[...].astype(F32)).astype(BF16)
    signal_ref[...] = (back * ig_ref[...].astype(F32)).astype(BF16)

    for k, (send, count) in enumerate(
        ((b_send, nj), (w_send, nz), (a_send, nz), (a2_send, nz), (g_send, nz), (b2_send, nj))
    ):
        wait_all(send, count - 1, send_sems.at[k])


def solution(mesh):
    nz = mesh.shape["ctx"]
    nj = mesh.shape["ch"]

    def local(out_gate, in_gate, signal, cotangent, filters, block_ids):
        tokens, width = out_gate.shape
        nf = filters.shape[1]
        nr = nf // nz
        vmem = pl.BlockSpec(memory_space=pltpu.VMEM)
        grad = jax.ShapeDtypeStruct((tokens, width), BF16)
        lag = pltpu.VMEM((nz, 8, SPAN), F32)
        by_ch = pltpu.VMEM((nj, 2, nf, SPAN), BF16)
        by_ctx = pltpu.VMEM((nz, 2, nr, nj, SPAN), BF16)
        return pl.pallas_call(
            partial(kernel, nz, nj, nf),
            out_shape=(grad, grad, grad, jax.ShapeDtypeStruct(filters.shape, F32)),
            in_specs=[pl.BlockSpec(memory_space=pltpu.SMEM)] + [vmem] * 5,
            out_specs=(vmem,) * 4,
            scratch_shapes=[
                lag,
                lag,
                by_ch,
                by_ch,
                by_ctx,
                by_ctx,
                by_ctx,
                by_ctx,
                by_ch,
                by_ch,
                lag,
                lag,
                pltpu.SemaphoreType.DMA((6,)),
                pltpu.SemaphoreType.DMA((6,)),
            ],
            compiler_params=pltpu.CompilerParams(
                collective_id=0, has_side_effects=True, vmem_limit_bytes=48 * 1024 * 1024
            ),
        )(block_ids, out_gate, in_gate, signal, cotangent, filters)

    return jax.shard_map(
        local,
        mesh=mesh,
        in_specs=(P("ctx", "ch"),) * 5 + (P("ctx"),),
        out_specs=(P("ctx", "ch"),) * 4,
        check_vma=False,
    )
```

```python
from functools import partial

import jax
import jax.numpy as jnp
import numpy as np
from jax import lax
from jax.experimental import pallas as pl
from jax.experimental.pallas import tpu as pltpu
from jax.sharding import PartitionSpec as P

MESH = pl.DeviceIdType.MESH
BF16 = jnp.bfloat16
F32 = jnp.float32
HALF = 64
SPAN = 128
FREQ = 128


def iota(shape, dim):
    return lax.broadcasted_iota(jnp.int32, shape, dim)


def dft_table():
    angle = np.pi * np.outer(np.arange(SPAN), 2 * np.arange(FREQ) + 1) / (2 * SPAN)
    full = np.concatenate([np.cos(angle), -np.sin(angle)], axis=1)
    high = full.astype(BF16)
    low = (full - high.astype(np.float64)).astype(BF16)
    return np.concatenate([high, low], axis=0)


def mm(left, right):
    return jnp.dot(left, right, preferred_element_type=F32)


def mm_nt(left, right):
    return lax.dot_general(left, right, (((1,), (1,)), ((), ())), preferred_element_type=F32)


def wait_bytes(ref, start, count, sem):
    view = ref.at[pl.ds(start, count)]
    pltpu.make_async_copy(view, view, sem).wait()


def split(values):
    high = values.astype(BF16)
    return high, (values - high.astype(F32)).astype(BF16)


def exchange_kernel(
    nz,
    nj,
    nf,
    ids_hbm,
    og_hbm,
    ig_hbm,
    sg_hbm,
    ct_hbm,
    fl_hbm,
    dft_hbm,
    conv_ref,
    back_ref,
    fgrad_ref,
    ig_ref,
    sg_ref,
    ct_ref,
    og_ref,
    dft_ref,
    ids_ref,
    ids_all,
    f_send,
    f_recv,
    a_send,
    a_recv,
    r_send,
    r_recv,
    g_send,
    g_recv,
    halves,
    spec,
    wspec,
    load_sems,
    send_sems,
    recv_sems,
):
    nc = 2 * nf
    nx = nj // 4
    zi = lax.axis_index("ctx")
    ji = lax.axis_index("ch")
    depth, core = zi // 2, zi % 2
    xi, yi = ji // 4, ji % 4

    def chunk_of(q):
        return 2 * lax.rem(xi + q // 2 + nx // 2, nx) + lax.rem(q + yi // 2, 2)

    def user_of(j):
        z = lax.rem(xi + nx - j // 4 + nx // 2, nx)
        return 2 * z + lax.rem(yi // 2 + j % 4 // 2, 2)

    mine = chunk_of(zi)

    loads = [
        pltpu.make_async_copy(src, dst, load_sems.at[k])
        for k, (src, dst) in enumerate(
            (
                (fl_hbm, f_send),
                (ig_hbm, ig_ref),
                (sg_hbm, sg_ref),
                (ct_hbm, ct_ref),
                (og_hbm, og_ref),
                (dft_hbm, dft_ref),
                (ids_hbm, ids_ref),
            )
        )
    ]
    for load in loads:
        load.start()

    barrier = pltpu.get_barrier_semaphore()

    def greet(device):
        pl.semaphore_signal(barrier, inc=1, device_id=device, device_id_type=MESH)

    owners = [(lax.rem(zi + s, nz), 2 * mine + r) for s in range(nz) for r in range(2)]
    users = []
    for s in range(nj):
        j = lax.rem(ji + s, nj)
        users.append((user_of(j), j))
    group = [lax.rem(zi + s, nz) for s in range(1, nz)]
    own = user_of(ji) == zi
    own_side = [2 * mine + r == ji for r in range(2)]

    for r in range(2):
        pl.when(jnp.logical_not(own_side[r]))(partial(greet, owners[r]))
    for device in owners[2:]:
        greet(device)
    for q in group:
        greet((q, ji))
    pl.when(jnp.logical_not(own))(partial(greet, users[0]))
    for device in users[1:]:
        greet(device)

    loads[0].wait()
    loads[1].wait()
    loads[2].wait()
    product = ig_ref[...].astype(F32) * sg_ref[...].astype(F32)
    a_send[:, 0] = product.T.astype(BF16).reshape(nz, nc, SPAN)
    loads[3].wait()
    loads[4].wait()
    weighted = ct_ref[...].astype(F32) * og_ref[...].astype(F32)
    a_send[:, 1] = weighted.T.astype(BF16).reshape(nz, nc, SPAN)

    pl.semaphore_wait(barrier, nz - 1 + 2 * nj - jnp.where(own, 2, 0))

    def remote(src, dst, k, device):
        return pltpu.make_async_remote_copy(
            src, dst, send_sems.at[k], recv_sems.at[k], device, MESH
        )

    f_slot = f_recv.at[zi, yi % 2]

    @pl.when(own)
    def _():
        pltpu.make_async_copy(f_send, f_slot, recv_sems.at[0]).start()

    @pl.when(jnp.logical_not(own))
    def _():
        remote(f_send, f_slot, 0, users[0]).start()

    for device in users[1:]:
        remote(f_send, f_slot, 0, device).start()

    loads[6].wait()
    for q in group:
        remote(ids_ref, ids_all.at[zi], 1, (q, ji)).start()
        remote(a_send.at[chunk_of(q)], a_recv.at[zi], 2, (q, ji)).start()
    ids_all[zi, 0] = ids_ref[0]
    ids_all[zi, 1] = ids_ref[1]
    a_recv[zi] = a_send[mine]

    wait_bytes(ids_all, 0, nz - 1, recv_sems.at[1])
    ids = [ids_all[s // 2, s % 2] for s in range(2 * nz)]
    order = []
    for n in range(2 * nz):
        place = jnp.int32(0)
        for s in range(2 * nz):
            place = jnp.where(ids[s] == n, s, place)
        order.append(place)

    loads[5].wait()
    table = dft_ref[...]
    low = iota((2 * nc, SPAN), 1) < HALF
    odd = iota((nc, FREQ), 1) % 2 == 1
    sign = jnp.where(odd, -1.0, 1.0)

    def spread(slot, values):
        turned = pltpu.roll(values, HALF, 1)
        halves[2 * slot] = jnp.where(low, values, turned)
        halves[2 * slot + 1] = jnp.where(low, turned, values)

    def pick(first, second):
        return jnp.where(low, halves[first], halves[second])

    wait_bytes(a_recv, 0, nz - 1, recv_sems.at[2])
    for z in range(nz):
        spread(z, a_recv[z].reshape(2 * nc, SPAN).astype(F32))
    blocks = [pick(order[2 * i], order[2 * i + 1]).astype(BF16) for i in range(nz)]
    blocks = jnp.concatenate(blocks, axis=0)
    spec[...] = mm(jnp.concatenate([blocks, blocks], axis=1), table).reshape(
        nz, 2, nc, 2 * FREQ
    )

    def part(ref, *at):
        value = ref[at]
        return value[:, :FREQ], value[:, FREQ:]

    def times(total, left, right):
        (a, b), (c, d) = left, right
        re, im = a * c - b * d, a * d + b * c
        return (re, im) if total is None else (total[0] + re, total[1] + im)

    def against(total, left, right):
        (a, b), (c, d) = left, right
        re, im = a * c + b * d, a * d - b * c
        return (re, im) if total is None else (total[0] + re, total[1] + im)

    cross = [None] * (nz + 1)
    for d in range(nz):
        for i in range(nz - d):
            cross[d] = against(cross[d], part(spec, i, 0), part(spec, i + d, 1))
    rows = []
    for d in range(nz):
        re, im = cross[d]
        if d + 1 < nz:
            re = re + sign * cross[d + 1][1]
            im = im - sign * cross[d + 1][0]
        rows.append(jnp.concatenate([re, im], axis=1))
    high, rest = split(jnp.concatenate(rows, axis=0))
    lags = mm_nt(high, table)
    lags = lags[:, :SPAN] + lags[:, SPAN:] + mm_nt(rest, table[:SPAN])
    g_send[...] = (lags * (1.0 / SPAN)).reshape(nz, 2, nf, SPAN)

    g_slot = g_recv.at[ji]
    for r in range(2):
        src = g_send.at[zi, r]

        def keep(src=src):
            pltpu.make_async_copy(src, g_slot, recv_sems.at[3]).start()

        def pass_on(src=src, r=r):
            remote(src, g_slot, 3, owners[r]).start()

        pl.when(own_side[r])(keep)
        pl.when(jnp.logical_not(own_side[r]))(pass_on)
    for s in range(1, nz):
        for r in range(2):
            z, j = owners[2 * s + r]
            remote(g_send.at[z, r], g_slot, 3, (z, j)).start()

    wait_bytes(f_recv, 0, nz, recv_sems.at[0])
    high, rest = split(f_recv[...].reshape(nz * nc, SPAN))
    raw = mm(jnp.concatenate([high, high], axis=1), table) + mm(rest, table[:SPAN])
    raw = raw.reshape(nz, nc, 2 * FREQ)
    for d in range(nz):
        re, im = raw[d, :, :FREQ], raw[d, :, FREQ:]
        if d:
            re = re - sign * raw[d - 1, :, FREQ:]
            im = im + sign * raw[d - 1, :, :FREQ]
        wspec[d, :, :FREQ] = re
        wspec[d, :, FREQ:] = im

    rows = []
    for m in range(nz):
        conv = back = None
        for i in range(m + 1):
            conv = times(conv, part(wspec, m - i), part(spec, i, 0))
        for j in range(m, nz):
            back = against(back, part(wspec, j - m), part(spec, j, 1))
        rows += [jnp.concatenate(conv, axis=1), jnp.concatenate(back, axis=1)]
    result = mm_nt(jnp.concatenate(rows, axis=0).astype(BF16), table)
    result = (result[:, :SPAN] + result[:, SPAN:]) * (1.0 / SPAN)
    for i in range(nz):
        spread(i, result[2 * nc * i : 2 * nc * (i + 1)])
    for z in range(nz):
        r_send[z] = pick(ids[2 * z], ids[2 * z + 1]).astype(BF16).reshape(2, nc, SPAN)
    for q in group:
        remote(r_send.at[q], r_recv.at[mine], 4, (q, ji)).start()
    r_recv[mine] = r_send[zi]

    wait_bytes(g_recv, 0, nj, recv_sems.at[3])
    total = g_recv[0]
    for j in range(1, nj):
        total = total + g_recv[j]
    fgrad_ref[...] = total

    wait_bytes(r_recv, 0, nz - 1, recv_sems.at[4])
    conv_ref[...] = r_recv[:, 0].reshape(nz * nc, SPAN)
    back_ref[...] = r_recv[:, 1].reshape(nz * nc, SPAN)

    wait_bytes(ids_all, 0, nz - 1, send_sems.at[1])
    wait_bytes(a_send, 0, nz - 1, send_sems.at[2])
    wait_bytes(r_send, 0, nz - 1, send_sems.at[4])

    @pl.when(own)
    def _():
        wait_bytes(g_recv, 0, nj - 1, send_sems.at[0])
        wait_bytes(g_recv, 0, nj - 1, send_sems.at[3])

    @pl.when(jnp.logical_not(own))
    def _():
        wait_bytes(g_recv, 0, nj, send_sems.at[0])
        wait_bytes(g_recv, 0, nj, send_sems.at[3])


def gate_kernel(
    conv_ref,
    back_ref,
    fgrad_ref,
    ig_ref,
    sg_ref,
    ct_ref,
    outer_hbm,
    inner_hbm,
    signal_hbm,
    fgrad_hbm,
    outer,
    inner,
    signal,
    sems,
):
    def put(src, dst, k):
        copy = pltpu.make_async_copy(src, dst, sems.at[k])
        copy.start()
        return copy

    copies = [put(fgrad_ref, fgrad_hbm, 0)]
    conv = conv_ref[...].astype(F32).T
    outer[...] = (ct_ref[...].astype(F32) * conv).astype(BF16)
    copies.append(put(outer, outer_hbm, 1))
    back = back_ref[...].astype(F32).T
    inner[...] = (back * sg_ref[...].astype(F32)).astype(BF16)
    copies.append(put(inner, inner_hbm, 2))
    signal[...] = (back * ig_ref[...].astype(F32)).astype(BF16)
    copies.append(put(signal, signal_hbm, 3))
    for copy in copies:
        copy.wait()


def solution(mesh):
    nz = mesh.shape["ctx"]
    nj = mesh.shape["ch"]

    def local(out_gate, in_gate, signal, cotangent, filters, block_ids):
        tokens, width = out_gate.shape
        nf = filters.shape[1]
        nc = 2 * nf
        vmem = pl.BlockSpec(memory_space=pltpu.VMEM)
        anywhere = pl.BlockSpec(memory_space=pltpu.HBM)
        grad = jax.ShapeDtypeStruct((tokens, width), BF16)
        turned = jax.ShapeDtypeStruct((width, tokens), BF16)
        tokens_vmem = pltpu.VMEM((tokens, width), BF16)
        block = pltpu.VMEM((nz, 2, nc, SPAN), BF16)
        held = pl.pallas_call(
            partial(exchange_kernel, nz, nj, nf),
            out_shape=(turned, turned, jax.ShapeDtypeStruct((nf, SPAN), F32), grad, grad, grad),
            in_specs=[anywhere] * 7,
            out_specs=(vmem,) * 6,
            scratch_shapes=[
                tokens_vmem,
                pltpu.VMEM((2 * SPAN, 2 * FREQ), BF16),
                pltpu.SMEM((2,), jnp.int32),
                pltpu.SMEM((nz, 2), jnp.int32),
                pltpu.VMEM((nf, SPAN), F32),
                pltpu.VMEM((nz, 2, nf, SPAN), F32),
                block,
                block,
                block,
                block,
                pltpu.VMEM((nz, 2, nf, SPAN), F32),
                pltpu.VMEM((nj, nf, SPAN), F32),
                pltpu.VMEM((2 * nz, 2 * nc, SPAN), F32),
                pltpu.VMEM((nz, 2, nc, 2 * FREQ), F32),
                pltpu.VMEM((nz, nc, 2 * FREQ), F32),
                pltpu.SemaphoreType.DMA((7,)),
                pltpu.SemaphoreType.DMA((5,)),
                pltpu.SemaphoreType.DMA((5,)),
            ],
            compiler_params=pltpu.CompilerParams(
                collective_id=0, has_side_effects=True, vmem_limit_bytes=48 * 1024 * 1024
            ),
        )(
            *(
                pltpu.with_memory_space_constraint(value, pltpu.HBM)
                for value in (
                    block_ids,
                    out_gate,
                    in_gate,
                    signal,
                    cotangent,
                    filters.T,
                    jnp.asarray(dft_table()),
                )
            ),
        )
        *grads, fgrad = pl.pallas_call(
            gate_kernel,
            out_shape=(grad, grad, grad, jax.ShapeDtypeStruct((nf, SPAN), F32)),
            in_specs=[vmem] * 6,
            out_specs=(anywhere,) * 4,
            scratch_shapes=[tokens_vmem] * 3 + [pltpu.SemaphoreType.DMA((4,))],
            compiler_params=pltpu.CompilerParams(vmem_limit_bytes=32 * 1024 * 1024),
        )(*held)
        return (*grads, fgrad.T)

    return jax.shard_map(
        local,
        mesh=mesh,
        in_specs=(P("ctx", "ch"),) * 5 + (P("ctx"),),
        out_specs=(P("ctx", "ch"),) * 4,
        check_vma=False,
    )
```

```python
from functools import partial

import jax
import jax.numpy as jnp
import numpy as np
from jax import lax
from jax.experimental import pallas as pl
from jax.experimental.pallas import tpu as pltpu
from jax.sharding import PartitionSpec as P

MESH = pl.DeviceIdType.MESH
BF16 = jnp.bfloat16
F32 = jnp.float32
HALF = 64
SPAN = 128
FREQ = 128


def iota(shape, dim):
    return lax.broadcasted_iota(jnp.int32, shape, dim)


def dft_table():
    angle = np.pi * np.outer(np.arange(SPAN), 2 * np.arange(FREQ) + 1) / (2 * SPAN)
    full = np.concatenate([np.cos(angle), -np.sin(angle)], axis=1)
    high = full.astype(BF16)
    low = (full - high.astype(np.float64)).astype(BF16)
    return np.concatenate([high, low], axis=0)


def mm(left, right):
    return jnp.dot(left, right, preferred_element_type=F32)


def mm_nt(left, right):
    return lax.dot_general(left, right, (((1,), (1,)), ((), ())), preferred_element_type=F32)


def wait_bytes(ref, start, count, sem):
    view = ref.at[pl.ds(start, count)]
    pltpu.make_async_copy(view, view, sem).wait()


def split(values):
    high = values.astype(BF16)
    return high, (values - high.astype(F32)).astype(BF16)


def exchange_kernel(
    nz,
    nj,
    nf,
    ids_hbm,
    og_hbm,
    ig_hbm,
    sg_hbm,
    ct_hbm,
    fl_hbm,
    dft_hbm,
    conv_ref,
    back_ref,
    fgrad_ref,
    ig_ref,
    sg_ref,
    ct_ref,
    og_ref,
    dft_ref,
    ids_ref,
    ids_all,
    fl_ref,
    f_send,
    f_recv,
    a_send,
    a_recv,
    r_send,
    r_recv,
    g_send,
    g_recv,
    halves,
    spec,
    wspec,
    load_sems,
    send_sems,
    recv_sems,
):
    nc = 2 * nf
    nx = nj // 4
    zi = lax.axis_index("ctx")
    ji = lax.axis_index("ch")
    depth, core = zi // 2, zi % 2
    xi, yi = ji // 4, ji % 4

    def chunk_of(q):
        return 2 * lax.rem(xi + q // 2 + nx // 2, nx) + lax.rem(q + yi // 2, 2)

    def user_of(j):
        z = lax.rem(xi + nx - j // 4 + nx // 2, nx)
        return 2 * z + lax.rem(yi // 2 + j % 4 // 2, 2)

    mine = chunk_of(zi)

    loads = [
        pltpu.make_async_copy(src, dst, load_sems.at[k])
        for k, (src, dst) in enumerate(
            (
                (ig_hbm, ig_ref),
                (sg_hbm, sg_ref),
                (ct_hbm, ct_ref),
                (og_hbm, og_ref),
                (dft_hbm, dft_ref),
                (fl_hbm, fl_ref),
                (ids_hbm, ids_ref),
            )
        )
    ]
    for load in loads:
        load.start()

    barrier = pltpu.get_barrier_semaphore()

    def greet(device):
        pl.semaphore_signal(barrier, inc=1, device_id=device, device_id_type=MESH)

    def hops(step, size):
        return min(step, size - step)

    nd = nz // 2
    steps = sorted(
        ((dz, dc) for dz in range(nd) for dc in range(2)),
        key=lambda s: (-hops(s[0], nd), -s[1]),
    )
    ctx_order = [2 * lax.rem(depth + dz, nd) + lax.rem(core + dc, 2) for dz, dc in steps]
    group = ctx_order[:-1]
    owners = [(z, 2 * mine + r) for z in ctx_order for r in range(2)]
    users = []
    for dx, dy in sorted(
        ((dx, dy) for dx in range(nx) for dy in range(4)),
        key=lambda s: -hops(s[0], nx) - hops(s[1], 4),
    ):
        j = 4 * lax.rem(xi + dx, nx) + lax.rem(yi + dy, 4)
        users.append((user_of(j), j))
    own = user_of(ji) == zi

    def gray(value):
        return value ^ (value >> 1)

    rank = 2 * gray(depth) + 1 - core
    first = [2 * gray(k // 2) + 1 - k % 2 for k in range(nz)]
    urgent = [
        jnp.where(rank <= k, first[k + 1], first[k]) for k in range(nz - 1)
    ]
    own_side = [2 * mine + r == ji for r in range(2)]

    for device in owners[:-2]:
        greet(device)
    for r in range(2):
        pl.when(jnp.logical_not(own_side[r]))(partial(greet, owners[r - 2]))
    for q in group:
        greet((q, ji))
    for step in range(1, nj):
        greet((zi, lax.rem(ji + step, nj)))

    loads[5].wait()
    f_send[...] = fl_ref[...].astype(BF16)
    loads[0].wait()
    loads[1].wait()
    product = ig_ref[...].astype(F32) * sg_ref[...].astype(F32)
    a_send[:, 0] = product.T.astype(BF16).reshape(nz, nc, SPAN)
    loads[2].wait()
    loads[3].wait()
    weighted = ct_ref[...].astype(F32) * og_ref[...].astype(F32)
    a_send[:, 1] = weighted.T.astype(BF16).reshape(nz, nc, SPAN)

    pl.semaphore_wait(barrier, nz - 2 + 2 * nj - jnp.where(own, 1, 0))

    def remote(src, dst, k, device):
        return pltpu.make_async_remote_copy(
            src, dst, send_sems.at[k], recv_sems.at[k], device, MESH
        )

    f_slot = f_recv.at[zi, yi % 2]
    for device in users[:-1]:
        remote(f_send, f_slot, 0, device).start()

    @pl.when(own)
    def _():
        pltpu.make_async_copy(f_send, f_slot, recv_sems.at[0]).start()

    @pl.when(jnp.logical_not(own))
    def _():
        remote(f_send, f_slot, 0, users[-1]).start()

    loads[6].wait()
    for q in group:
        remote(ids_ref, ids_all.at[zi], 1, (q, ji)).start()
        remote(a_send.at[chunk_of(q)], a_recv.at[zi], 2, (q, ji)).start()
    ids_all[zi, 0] = ids_ref[0]
    ids_all[zi, 1] = ids_ref[1]
    a_recv[zi] = a_send[mine]

    wait_bytes(ids_all, 0, nz - 1, recv_sems.at[1])
    ids = [ids_all[s // 2, s % 2] for s in range(2 * nz)]
    order = []
    for n in range(2 * nz):
        place = jnp.int32(0)
        for s in range(2 * nz):
            place = jnp.where(ids[s] == n, s, place)
        order.append(place)

    loads[4].wait()
    table = dft_ref[...]
    low = iota((2 * nc, SPAN), 1) < HALF
    odd = iota((nc, FREQ), 1) % 2 == 1
    sign = jnp.where(odd, -1.0, 1.0)

    def spread(slot, values):
        turned = pltpu.roll(values, HALF, 1)
        halves[2 * slot] = jnp.where(low, values, turned)
        halves[2 * slot + 1] = jnp.where(low, turned, values)

    def pick(first, second):
        return jnp.where(low, halves[first], halves[second])

    wait_bytes(a_recv, 0, nz - 1, recv_sems.at[2])
    for z in range(nz):
        spread(z, a_recv[z].reshape(2 * nc, SPAN).astype(F32))
    blocks = [pick(order[2 * i], order[2 * i + 1]).astype(BF16) for i in range(nz)]
    blocks = jnp.concatenate(blocks, axis=0)
    spec[...] = mm(jnp.concatenate([blocks, blocks], axis=1), table).reshape(
        nz, 2, nc, 2 * FREQ
    )

    def part(ref, *at):
        value = ref[at]
        return value[:, :FREQ], value[:, FREQ:]

    def times(total, left, right):
        (a, b), (c, d) = left, right
        re, im = a * c - b * d, a * d + b * c
        return (re, im) if total is None else (total[0] + re, total[1] + im)

    def against(total, left, right):
        (a, b), (c, d) = left, right
        re, im = a * c + b * d, a * d - b * c
        return (re, im) if total is None else (total[0] + re, total[1] + im)

    cross = [None] * (nz + 1)
    for d in range(nz):
        for i in range(nz - d):
            cross[d] = against(cross[d], part(spec, i, 0), part(spec, i + d, 1))
    rows = []
    for d in range(nz):
        re, im = cross[d]
        if d + 1 < nz:
            re = re + sign * cross[d + 1][1]
            im = im - sign * cross[d + 1][0]
        rows.append(jnp.concatenate([re, im], axis=1))
    high, rest = split(jnp.concatenate(rows, axis=0))
    lags = mm_nt(high, table)
    lags = lags[:, :SPAN] + lags[:, SPAN:] + mm_nt(rest, table[:SPAN])
    g_send[...] = (lags * (1.0 / SPAN)).astype(BF16).reshape(nz, 2, nf, SPAN)

    g_slot = g_recv.at[ji]
    near = ji % 2
    for k in range(nz):
        z = first[k]
        remote(g_send.at[z, 1 - near], g_slot, 3, (z, 2 * mine + 1 - near)).start()
        if k < nz - 1:
            z = urgent[k]
            remote(g_send.at[z, near], g_slot, 3, (z, 2 * mine + near)).start()

    @pl.when(own)
    def _():
        pltpu.make_async_copy(g_send.at[zi, near], g_slot, recv_sems.at[3]).start()

    @pl.when(jnp.logical_not(own))
    def _():
        remote(g_send.at[zi, near], g_slot, 3, (zi, 2 * mine + near)).start()

    wait_bytes(f_recv, 0, nz, recv_sems.at[0])

    taps = f_recv[...].reshape(nz * nc, SPAN)
    raw = mm(jnp.concatenate([taps, taps], axis=1), table)
    raw = raw.reshape(nz, nc, 2 * FREQ)
    for d in range(nz):
        re, im = raw[d, :, :FREQ], raw[d, :, FREQ:]
        if d:
            re = re - sign * raw[d - 1, :, FREQ:]
            im = im + sign * raw[d - 1, :, :FREQ]
        wspec[d, :, :FREQ] = re
        wspec[d, :, FREQ:] = im

    rows = []
    for m in range(nz):
        conv = back = None
        for i in range(m + 1):
            conv = times(conv, part(wspec, m - i), part(spec, i, 0))
        for j in range(m, nz):
            back = against(back, part(wspec, j - m), part(spec, j, 1))
        rows += [jnp.concatenate(conv, axis=1), jnp.concatenate(back, axis=1)]
    result = mm_nt(jnp.concatenate(rows, axis=0).astype(BF16), table)
    result = (result[:, :SPAN] + result[:, SPAN:]) * (1.0 / SPAN)
    for i in range(nz):
        spread(i, result[2 * nc * i : 2 * nc * (i + 1)])
    for z in range(nz):
        r_send[z] = pick(ids[2 * z], ids[2 * z + 1]).astype(BF16).reshape(2, nc, SPAN)
    for q in urgent:
        remote(r_send.at[q], r_recv.at[mine], 4, (q, ji)).start()
    r_recv[mine] = r_send[zi]

    wait_bytes(g_recv, 0, nj, recv_sems.at[3])
    total = g_recv[0].astype(F32)
    for j in range(1, nj):
        total = total + g_recv[j].astype(F32)
    fgrad_ref[...] = total

    wait_bytes(r_recv, 0, nz - 1, recv_sems.at[4])
    conv_ref[...] = r_recv[:, 0].reshape(nz * nc, SPAN)
    back_ref[...] = r_recv[:, 1].reshape(nz * nc, SPAN)

    wait_bytes(ids_all, 0, nz - 1, send_sems.at[1])
    wait_bytes(a_send, 0, nz - 1, send_sems.at[2])
    wait_bytes(r_send, 0, nz - 1, send_sems.at[4])

    @pl.when(own)
    def _():
        wait_bytes(f_recv.reshape(nj, nf, SPAN), 0, nj - 1, send_sems.at[0])
        wait_bytes(g_recv, 0, nj - 1, send_sems.at[3])

    @pl.when(jnp.logical_not(own))
    def _():
        wait_bytes(f_recv, 0, nz, send_sems.at[0])
        wait_bytes(g_recv, 0, nj, send_sems.at[3])


def gate_kernel(
    conv_ref,
    back_ref,
    fgrad_ref,
    ig_ref,
    sg_ref,
    ct_ref,
    outer_hbm,
    inner_hbm,
    signal_hbm,
    fgrad_hbm,
    outer,
    inner,
    signal,
    sems,
):
    def put(src, dst, k):
        copy = pltpu.make_async_copy(src, dst, sems.at[k])
        copy.start()
        return copy

    copies = [put(fgrad_ref, fgrad_hbm, 0)]
    conv = conv_ref[...].astype(F32).T
    outer[...] = (ct_ref[...].astype(F32) * conv).astype(BF16)
    copies.append(put(outer, outer_hbm, 1))
    back = back_ref[...].astype(F32).T
    inner[...] = (back * sg_ref[...].astype(F32)).astype(BF16)
    copies.append(put(inner, inner_hbm, 2))
    signal[...] = (back * ig_ref[...].astype(F32)).astype(BF16)
    copies.append(put(signal, signal_hbm, 3))
    for copy in copies:
        copy.wait()


def solution(mesh):
    nz = mesh.shape["ctx"]
    nj = mesh.shape["ch"]

    def local(out_gate, in_gate, signal, cotangent, filters, block_ids):
        tokens, width = out_gate.shape
        nf = filters.shape[1]
        nc = 2 * nf
        vmem = pl.BlockSpec(memory_space=pltpu.VMEM)
        anywhere = pl.BlockSpec(memory_space=pltpu.HBM)
        grad = jax.ShapeDtypeStruct((tokens, width), BF16)
        turned = jax.ShapeDtypeStruct((width, tokens), BF16)
        tokens_vmem = pltpu.VMEM((tokens, width), BF16)
        block = pltpu.VMEM((nz, 2, nc, SPAN), BF16)
        held = pl.pallas_call(
            partial(exchange_kernel, nz, nj, nf),
            out_shape=(turned, turned, jax.ShapeDtypeStruct((nf, SPAN), F32), grad, grad, grad),
            in_specs=[anywhere] * 7,
            out_specs=(vmem,) * 6,
            scratch_shapes=[
                tokens_vmem,
                pltpu.VMEM((2 * SPAN, 2 * FREQ), BF16),
                pltpu.SMEM((2,), jnp.int32),
                pltpu.SMEM((nz, 2), jnp.int32),
                pltpu.VMEM((nf, SPAN), F32),
                pltpu.VMEM((nf, SPAN), BF16),
                pltpu.VMEM((nz, 2, nf, SPAN), BF16),
                block,
                block,
                block,
                block,
                pltpu.VMEM((nz, 2, nf, SPAN), BF16),
                pltpu.VMEM((nj, nf, SPAN), BF16),
                pltpu.VMEM((2 * nz, 2 * nc, SPAN), F32),
                pltpu.VMEM((nz, 2, nc, 2 * FREQ), F32),
                pltpu.VMEM((nz, nc, 2 * FREQ), F32),
                pltpu.SemaphoreType.DMA((7,)),
                pltpu.SemaphoreType.DMA((5,)),
                pltpu.SemaphoreType.DMA((5,)),
            ],
            compiler_params=pltpu.CompilerParams(
                collective_id=0, has_side_effects=True, vmem_limit_bytes=48 * 1024 * 1024
            ),
        )(
            *(
                pltpu.with_memory_space_constraint(value, pltpu.HBM)
                for value in (
                    block_ids,
                    out_gate,
                    in_gate,
                    signal,
                    cotangent,
                    filters.T,
                    jnp.asarray(dft_table()),
                )
            ),
        )
        *grads, fgrad = pl.pallas_call(
            gate_kernel,
            out_shape=(grad, grad, grad, jax.ShapeDtypeStruct((nf, SPAN), F32)),
            in_specs=[vmem] * 6,
            out_specs=(anywhere,) * 4,
            scratch_shapes=[tokens_vmem] * 3 + [pltpu.SemaphoreType.DMA((4,))],
            compiler_params=pltpu.CompilerParams(vmem_limit_bytes=32 * 1024 * 1024),
        )(*held)
        return (*grads, fgrad.T)

    return jax.shard_map(
        local,
        mesh=mesh,
        in_specs=(P("ctx", "ch"),) * 5 + (P("ctx"),),
        out_specs=(P("ctx", "ch"),) * 4,
        check_vma=False,
    )
```

```python
from functools import partial

import jax
import jax.numpy as jnp
import numpy as np
from jax import lax
from jax.experimental import pallas as pl
from jax.experimental.pallas import tpu as pltpu
from jax.sharding import PartitionSpec as P

MESH = pl.DeviceIdType.MESH
BF16 = jnp.bfloat16
F32 = jnp.float32
HALF = 64
SPAN = 128
FREQ = 128


def iota(shape, dim):
    return lax.broadcasted_iota(jnp.int32, shape, dim)


def dft_table():
    angle = np.pi * np.outer(np.arange(SPAN), 2 * np.arange(FREQ) + 1) / (2 * SPAN)
    full = np.concatenate([np.cos(angle), -np.sin(angle)], axis=1)
    high = full.astype(BF16)
    low = (full - high.astype(np.float64)).astype(BF16)
    return np.concatenate([high, low], axis=0)


def mm(left, right):
    return jnp.dot(left, right, preferred_element_type=F32)


def mm_nt(left, right):
    return lax.dot_general(left, right, (((1,), (1,)), ((), ())), preferred_element_type=F32)


def wait_bytes(ref, start, count, sem):
    view = ref.at[pl.ds(start, count)]
    pltpu.make_async_copy(view, view, sem).wait()


def split(values):
    high = values.astype(BF16)
    return high, (values - high.astype(F32)).astype(BF16)


def exchange_kernel(
    nz,
    nj,
    nf,
    ids_hbm,
    og_hbm,
    ig_hbm,
    sg_hbm,
    ct_hbm,
    fl_hbm,
    dft_hbm,
    conv_ref,
    back_ref,
    fgrad_ref,
    ig_ref,
    sg_ref,
    ct_ref,
    og_ref,
    dft_ref,
    ids_ref,
    ids_all,
    fl_ref,
    f_send,
    f_recv,
    a_send,
    a_recv,
    r_send,
    r_recv,
    g_send,
    g_recv,
    halves,
    spec,
    wspec,
    load_sems,
    send_sems,
    recv_sems,
):
    nc = 2 * nf
    nx = nj // 4
    zi = lax.axis_index("ctx")
    ji = lax.axis_index("ch")
    depth, core = zi // 2, zi % 2
    xi, yi = ji // 4, ji % 4

    def chunk_of(q):
        return 2 * lax.rem(xi + q // 2 + 1, nx) + lax.rem(q + yi // 2, 2)

    def user_of(j):
        z = lax.rem(xi + 2 * nx - j // 4 - 1, nx)
        return 2 * z + lax.rem(yi // 2 + j % 4 // 2, 2)

    mine = chunk_of(zi)

    barrier = pltpu.get_barrier_semaphore()

    def greet(device):
        pl.semaphore_signal(barrier, inc=1, device_id=device, device_id_type=MESH)

    def hops(step, size):
        return min(step, size - step)

    nd = nz // 2
    steps = sorted(
        ((dz, dc) for dz in range(nd) for dc in range(2)),
        key=lambda s: (-hops(s[0], nd), -s[1]),
    )
    ctx_order = [2 * lax.rem(depth + dz, nd) + lax.rem(core + dc, 2) for dz, dc in steps]
    group = ctx_order[:-1]
    owners = [(z, 2 * mine + r) for z in ctx_order for r in range(2)]
    users = []
    for dx, dy in sorted(
        ((dx, dy) for dx in range(nx) for dy in range(4)),
        key=lambda s: -hops(s[0], nx) - hops(s[1], 4),
    ):
        j = 4 * lax.rem(xi + dx, nx) + lax.rem(yi + dy, 4)
        users.append((user_of(j), j))
    own = user_of(ji) == zi

    def gray(value):
        return value ^ (value >> 1)

    rank = 2 * gray(depth) + 1 - core
    first = [2 * gray(k // 2) + 1 - k % 2 for k in range(nz)]
    urgent = [
        jnp.where(rank <= k, first[k + 1], first[k]) for k in range(nz - 1)
    ]
    own_side = [2 * mine + r == ji for r in range(2)]

    for device in owners[:-2]:
        greet(device)
    for r in range(2):
        pl.when(jnp.logical_not(own_side[r]))(partial(greet, owners[r - 2]))
    for q in group:
        greet((q, ji))
    for step in range(1, nj):
        greet((zi, lax.rem(ji + step, nj)))

    loads = [
        pltpu.make_async_copy(src, dst, load_sems.at[k])
        for k, (src, dst) in enumerate(
            (
                (ig_hbm, ig_ref),
                (sg_hbm, sg_ref),
                (ct_hbm, ct_ref),
                (og_hbm, og_ref),
                (dft_hbm, dft_ref),
                (fl_hbm, fl_ref),
                (ids_hbm, ids_ref),
            )
        )
    ]
    for load in loads:
        load.start()

    loads[5].wait()
    f_send[...] = fl_ref[...].astype(BF16)
    loads[0].wait()
    loads[1].wait()
    product = ig_ref[...].astype(F32) * sg_ref[...].astype(F32)
    a_send[:, 0] = product.T.astype(BF16).reshape(nz, nc, SPAN)
    loads[2].wait()
    loads[3].wait()
    weighted = ct_ref[...].astype(F32) * og_ref[...].astype(F32)
    a_send[:, 1] = weighted.T.astype(BF16).reshape(nz, nc, SPAN)

    pl.semaphore_wait(barrier, nz - 2 + 2 * nj - jnp.where(own, 1, 0))

    def remote(src, dst, k, device):
        return pltpu.make_async_remote_copy(
            src, dst, send_sems.at[k], recv_sems.at[k], device, MESH
        )

    f_slot = f_recv.at[zi, yi % 2]
    loads[6].wait()
    for device in users[:5]:
        remote(f_send, f_slot, 0, device).start()
    for q in group:
        remote(ids_ref, ids_all.at[zi], 1, (q, ji)).start()
        remote(a_send.at[chunk_of(q)], a_recv.at[zi], 2, (q, ji)).start()
    for device in users[5:-1]:
        remote(f_send, f_slot, 0, device).start()

    @pl.when(own)
    def _():
        pltpu.make_async_copy(f_send, f_slot, recv_sems.at[0]).start()

    @pl.when(jnp.logical_not(own))
    def _():
        remote(f_send, f_slot, 0, users[-1]).start()

    ids_all[zi, 0] = ids_ref[0]
    ids_all[zi, 1] = ids_ref[1]
    a_recv[zi] = a_send[mine]

    wait_bytes(ids_all, 0, nz - 1, recv_sems.at[1])
    ids = [ids_all[s // 2, s % 2] for s in range(2 * nz)]
    order = []
    for n in range(2 * nz):
        place = jnp.int32(0)
        for s in range(2 * nz):
            place = jnp.where(ids[s] == n, s, place)
        order.append(place)

    loads[4].wait()
    table = dft_ref[...]
    low = iota((2 * nc, SPAN), 1) < HALF
    odd = iota((nc, FREQ), 1) % 2 == 1
    sign = jnp.where(odd, -1.0, 1.0)

    def spread(slot, values):
        turned = pltpu.roll(values, HALF, 1)
        halves[2 * slot] = jnp.where(low, values, turned)
        halves[2 * slot + 1] = jnp.where(low, turned, values)

    def pick(first, second):
        return jnp.where(low, halves[first], halves[second])

    wait_bytes(a_recv, 0, nz - 1, recv_sems.at[2])
    for z in range(nz):
        spread(z, a_recv[z].reshape(2 * nc, SPAN).astype(F32))
    blocks = [pick(order[2 * i], order[2 * i + 1]).astype(BF16) for i in range(nz)]
    blocks = jnp.concatenate(blocks, axis=0)
    spec[...] = mm(jnp.concatenate([blocks, blocks], axis=1), table).reshape(
        nz, 2, nc, 2 * FREQ
    )

    def part(ref, *at):
        value = ref[at]
        return value[:, :FREQ], value[:, FREQ:]

    def times(total, left, right):
        (a, b), (c, d) = left, right
        re, im = a * c - b * d, a * d + b * c
        return (re, im) if total is None else (total[0] + re, total[1] + im)

    def against(total, left, right):
        (a, b), (c, d) = left, right
        re, im = a * c + b * d, a * d - b * c
        return (re, im) if total is None else (total[0] + re, total[1] + im)

    cross = [None] * (nz + 1)
    for d in range(nz):
        for i in range(nz - d):
            cross[d] = against(cross[d], part(spec, i, 0), part(spec, i + d, 1))
    rows = []
    for d in range(nz):
        re, im = cross[d]
        if d + 1 < nz:
            re = re + sign * cross[d + 1][1]
            im = im - sign * cross[d + 1][0]
        rows.append(jnp.concatenate([re, im], axis=1))
    high, rest = split(jnp.concatenate(rows, axis=0))
    lags = mm_nt(high, table)
    lags = lags[:, :SPAN] + lags[:, SPAN:] + mm_nt(rest, table[:SPAN])
    g_send[...] = (lags * (1.0 / SPAN)).astype(BF16).reshape(nz, 2, nf, SPAN)

    g_slot = g_recv.at[ji]
    near = ji % 2
    for k in range(nz):
        z = first[k]
        remote(g_send.at[z, 1 - near], g_slot, 3, (z, 2 * mine + 1 - near)).start()
        if k < nz - 1:
            z = urgent[k]
            remote(g_send.at[z, near], g_slot, 3, (z, 2 * mine + near)).start()

    @pl.when(own)
    def _():
        pltpu.make_async_copy(g_send.at[zi, near], g_slot, recv_sems.at[3]).start()

    @pl.when(jnp.logical_not(own))
    def _():
        remote(g_send.at[zi, near], g_slot, 3, (zi, 2 * mine + near)).start()

    wait_bytes(f_recv, 0, nz, recv_sems.at[0])

    taps = f_recv[...].reshape(nz * nc, SPAN)
    raw = mm(jnp.concatenate([taps, taps], axis=1), table)
    raw = raw.reshape(nz, nc, 2 * FREQ)
    for d in range(nz):
        re, im = raw[d, :, :FREQ], raw[d, :, FREQ:]
        if d:
            re = re - sign * raw[d - 1, :, FREQ:]
            im = im + sign * raw[d - 1, :, :FREQ]
        wspec[d, :, :FREQ] = re
        wspec[d, :, FREQ:] = im

    rows = []
    for m in range(nz):
        conv = back = None
        for i in range(m + 1):
            conv = times(conv, part(wspec, m - i), part(spec, i, 0))
        for j in range(m, nz):
            back = against(back, part(wspec, j - m), part(spec, j, 1))
        rows += [jnp.concatenate(conv, axis=1), jnp.concatenate(back, axis=1)]
    result = mm_nt(jnp.concatenate(rows, axis=0).astype(BF16), table)
    result = (result[:, :SPAN] + result[:, SPAN:]) * (1.0 / SPAN)
    for i in range(nz):
        spread(i, result[2 * nc * i : 2 * nc * (i + 1)])
    for z in range(nz):
        r_send[z] = pick(ids[2 * z], ids[2 * z + 1]).astype(BF16).reshape(2, nc, SPAN)
    for q in urgent:
        remote(r_send.at[q], r_recv.at[mine], 4, (q, ji)).start()
    r_recv[mine] = r_send[zi]

    wait_bytes(g_recv, 0, nj, recv_sems.at[3])
    total = g_recv[0].astype(F32)
    for j in range(1, nj):
        total = total + g_recv[j].astype(F32)
    fgrad_ref[...] = total

    wait_bytes(r_recv, 0, nz - 1, recv_sems.at[4])
    conv_ref[...] = r_recv[:, 0].reshape(nz * nc, SPAN)
    back_ref[...] = r_recv[:, 1].reshape(nz * nc, SPAN)

    wait_bytes(ids_all, 0, nz - 1, send_sems.at[1])
    wait_bytes(a_send, 0, nz - 1, send_sems.at[2])
    wait_bytes(r_send, 0, nz - 1, send_sems.at[4])

    @pl.when(own)
    def _():
        wait_bytes(f_recv.reshape(nj, nf, SPAN), 0, nj - 1, send_sems.at[0])
        wait_bytes(g_recv, 0, nj - 1, send_sems.at[3])

    @pl.when(jnp.logical_not(own))
    def _():
        wait_bytes(f_recv, 0, nz, send_sems.at[0])
        wait_bytes(g_recv, 0, nj, send_sems.at[3])


def gate_kernel(
    conv_ref,
    back_ref,
    fgrad_ref,
    ig_ref,
    sg_ref,
    ct_ref,
    outer_hbm,
    inner_hbm,
    signal_hbm,
    fgrad_hbm,
    outer,
    inner,
    signal,
    sems,
):
    def put(src, dst, k):
        copy = pltpu.make_async_copy(src, dst, sems.at[k])
        copy.start()
        return copy

    copies = [put(fgrad_ref, fgrad_hbm, 0)]
    conv = conv_ref[...].astype(F32).T
    outer[...] = (ct_ref[...].astype(F32) * conv).astype(BF16)
    copies.append(put(outer, outer_hbm, 1))
    back = back_ref[...].astype(F32).T
    inner[...] = (back * sg_ref[...].astype(F32)).astype(BF16)
    copies.append(put(inner, inner_hbm, 2))
    signal[...] = (back * ig_ref[...].astype(F32)).astype(BF16)
    copies.append(put(signal, signal_hbm, 3))
    for copy in copies:
        copy.wait()


def solution(mesh):
    nz = mesh.shape["ctx"]
    nj = mesh.shape["ch"]

    def local(out_gate, in_gate, signal, cotangent, filters, block_ids):
        tokens, width = out_gate.shape
        nf = filters.shape[1]
        nc = 2 * nf
        vmem = pl.BlockSpec(memory_space=pltpu.VMEM)
        anywhere = pl.BlockSpec(memory_space=pltpu.HBM)
        grad = jax.ShapeDtypeStruct((tokens, width), BF16)
        turned = jax.ShapeDtypeStruct((width, tokens), BF16)
        tokens_vmem = pltpu.VMEM((tokens, width), BF16)
        block = pltpu.VMEM((nz, 2, nc, SPAN), BF16)
        held = pl.pallas_call(
            partial(exchange_kernel, nz, nj, nf),
            out_shape=(turned, turned, jax.ShapeDtypeStruct((nf, SPAN), F32), grad, grad, grad),
            in_specs=[anywhere] * 7,
            out_specs=(vmem,) * 6,
            scratch_shapes=[
                tokens_vmem,
                pltpu.VMEM((2 * SPAN, 2 * FREQ), BF16),
                pltpu.SMEM((2,), jnp.int32),
                pltpu.SMEM((nz, 2), jnp.int32),
                pltpu.VMEM((nf, SPAN), F32),
                pltpu.VMEM((nf, SPAN), BF16),
                pltpu.VMEM((nz, 2, nf, SPAN), BF16),
                block,
                block,
                block,
                block,
                pltpu.VMEM((nz, 2, nf, SPAN), BF16),
                pltpu.VMEM((nj, nf, SPAN), BF16),
                pltpu.VMEM((2 * nz, 2 * nc, SPAN), F32),
                pltpu.VMEM((nz, 2, nc, 2 * FREQ), F32),
                pltpu.VMEM((nz, nc, 2 * FREQ), F32),
                pltpu.SemaphoreType.DMA((7,)),
                pltpu.SemaphoreType.DMA((5,)),
                pltpu.SemaphoreType.DMA((5,)),
            ],
            compiler_params=pltpu.CompilerParams(
                collective_id=0, has_side_effects=True, vmem_limit_bytes=48 * 1024 * 1024
            ),
        )(
            *(
                pltpu.with_memory_space_constraint(value, pltpu.HBM)
                for value in (
                    block_ids,
                    out_gate,
                    in_gate,
                    signal,
                    cotangent,
                    filters.T,
                    jnp.asarray(dft_table()),
                )
            ),
        )
        *grads, fgrad = pl.pallas_call(
            gate_kernel,
            out_shape=(grad, grad, grad, jax.ShapeDtypeStruct((nf, SPAN), F32)),
            in_specs=[vmem] * 6,
            out_specs=(anywhere,) * 4,
            scratch_shapes=[tokens_vmem] * 3 + [pltpu.SemaphoreType.DMA((4,))],
            compiler_params=pltpu.CompilerParams(vmem_limit_bytes=32 * 1024 * 1024),
        )(*held)
        return (*grads, fgrad.T)

    return jax.shard_map(
        local,
        mesh=mesh,
        in_specs=(P("ctx", "ch"),) * 5 + (P("ctx"),),
        out_specs=(P("ctx", "ch"),) * 4,
        check_vma=False,
    )
```

```python
from functools import partial

import jax
import jax.numpy as jnp
import numpy as np
from jax import lax
from jax.experimental import pallas as pl
from jax.experimental.pallas import tpu as pltpu
from jax.sharding import PartitionSpec as P

MESH = pl.DeviceIdType.MESH
BF16 = jnp.bfloat16
F32 = jnp.float32
HALF = 64
SPAN = 128
FREQ = 128


def iota(shape, dim):
    return lax.broadcasted_iota(jnp.int32, shape, dim)


def dft_table():
    angle = np.pi * np.outer(np.arange(SPAN), 2 * np.arange(FREQ) + 1) / (2 * SPAN)
    full = np.concatenate([np.cos(angle), -np.sin(angle)], axis=1)
    high = full.astype(BF16)
    low = (full - high.astype(np.float64)).astype(BF16)
    return np.concatenate([high, low], axis=0)


def mm(left, right, nt=False, parts=4):
    dims = (((1,), (1 if nt else 0,)), ((), ()))
    step = left.shape[0] // parts
    return jnp.concatenate(
        [
            lax.dot_general(
                left[k * step : (k + 1) * step], right, dims, preferred_element_type=F32
            )
            for k in range(parts)
        ],
        axis=0,
    )


def mm_nt(left, right):
    return mm(left, right, nt=True)


def wait_bytes(ref, start, count, sem):
    view = ref.at[pl.ds(start, count)]
    pltpu.make_async_copy(view, view, sem).wait()


def split(values):
    high = values.astype(BF16)
    return high, (values - high.astype(F32)).astype(BF16)


def exchange_kernel(
    nz,
    nj,
    nf,
    ids_hbm,
    og_hbm,
    ig_hbm,
    sg_hbm,
    ct_hbm,
    fl_hbm,
    dft_hbm,
    conv_ref,
    back_ref,
    fgrad_ref,
    ig_ref,
    sg_ref,
    ct_ref,
    og_ref,
    dft_ref,
    ids_ref,
    ids_all,
    fl_ref,
    f_send,
    f_recv,
    a_send,
    a_recv,
    r_send,
    r_recv,
    g_send,
    g_recv,
    halves,
    spec,
    wspec,
    sums,
    load_sems,
    send_sems,
    recv_sems,
):
    nc = 2 * nf
    nx = nj // 4
    zi = lax.axis_index("ctx")
    ji = lax.axis_index("ch")
    depth, core = zi // 2, zi % 2
    xi, yi = ji // 4, ji % 4

    def chunk_of(q):
        return 2 * lax.rem(xi + q // 2 + 1, nx) + lax.rem(q + yi // 2, 2)

    def user_of(j):
        z = lax.rem(xi + 2 * nx - j // 4 - 1, nx)
        return 2 * z + lax.rem(yi // 2 + j % 4 // 2, 2)

    mine = chunk_of(zi)

    barrier = pltpu.get_barrier_semaphore()

    def greet(device):
        pl.semaphore_signal(barrier, inc=1, device_id=device, device_id_type=MESH)

    def hops(step, size):
        return min(step, size - step)

    nd = nz // 2
    steps = sorted(
        ((dz, dc) for dz in range(nd) for dc in range(2)),
        key=lambda s: (-hops(s[0], nd), -s[1]),
    )
    ctx_order = [2 * lax.rem(depth + dz, nd) + lax.rem(core + dc, 2) for dz, dc in steps]
    group = ctx_order[:-1]
    owners = [(z, 2 * mine + r) for z in ctx_order for r in range(2)]
    users = []
    for dx, dy in sorted(
        ((dx, dy) for dx in range(nx) for dy in range(4)),
        key=lambda s: -hops(s[0], nx) - hops(s[1], 4),
    ):
        j = 4 * lax.rem(xi + dx, nx) + lax.rem(yi + dy, 4)
        users.append((user_of(j), j))
    own = user_of(ji) == zi

    def gray(value):
        return value ^ (value >> 1)

    rank = 2 * gray(depth) + 1 - core
    first = [2 * gray(k // 2) + 1 - k % 2 for k in range(nz)]
    urgent = [
        jnp.where(rank <= k, first[k + 1], first[k]) for k in range(nz - 1)
    ]
    own_side = [2 * mine + r == ji for r in range(2)]

    for device in owners[:-2]:
        greet(device)
    for r in range(2):
        pl.when(jnp.logical_not(own_side[r]))(partial(greet, owners[r - 2]))
    for q in group:
        greet((q, ji))
    for step in range(1, nj):
        greet((zi, lax.rem(ji + step, nj)))

    loads = [
        pltpu.make_async_copy(src, dst, load_sems.at[k])
        for k, (src, dst) in enumerate(
            (
                (ig_hbm, ig_ref),
                (sg_hbm, sg_ref),
                (ct_hbm, ct_ref),
                (og_hbm, og_ref),
                (dft_hbm, dft_ref),
                (fl_hbm, fl_ref),
                (ids_hbm, ids_ref),
            )
        )
    ]
    for load in loads:
        load.start()

    loads[5].wait()
    f_send[...] = fl_ref[...].astype(BF16)
    loads[0].wait()
    loads[1].wait()
    product = ig_ref[...].astype(F32) * sg_ref[...].astype(F32)
    a_send[:, 0] = product.T.astype(BF16).reshape(nz, nc, SPAN)
    loads[2].wait()
    loads[3].wait()
    weighted = ct_ref[...].astype(F32) * og_ref[...].astype(F32)
    a_send[:, 1] = weighted.T.astype(BF16).reshape(nz, nc, SPAN)

    pl.semaphore_wait(barrier, nz - 2 + 2 * nj - jnp.where(own, 1, 0))

    def remote(src, dst, k, device):
        return pltpu.make_async_remote_copy(
            src, dst, send_sems.at[k], recv_sems.at[k], device, MESH
        )

    f_slot = f_recv.at[zi, yi % 2]
    loads[6].wait()
    for device in users[: nj // 4]:
        remote(f_send, f_slot, 0, device).start()
    for q in group:
        remote(ids_ref, ids_all.at[zi], 1, (q, ji)).start()
        remote(a_send.at[chunk_of(q)], a_recv.at[zi], 2, (q, ji)).start()
    for device in users[nj // 4 : -1]:
        remote(f_send, f_slot, 0, device).start()

    @pl.when(own)
    def _():
        pltpu.make_async_copy(f_send, f_slot, recv_sems.at[0]).start()

    @pl.when(jnp.logical_not(own))
    def _():
        remote(f_send, f_slot, 0, users[-1]).start()

    ids_all[zi, 0] = ids_ref[0]
    ids_all[zi, 1] = ids_ref[1]
    a_recv[zi] = a_send[mine]

    wait_bytes(ids_all, 0, nz - 1, recv_sems.at[1])
    ids = [ids_all[s // 2, s % 2] for s in range(2 * nz)]
    order = []
    for n in range(2 * nz):
        place = jnp.int32(0)
        for s in range(2 * nz):
            place = jnp.where(ids[s] == n, s, place)
        order.append(place)

    loads[4].wait()
    table = dft_ref[...]
    low = iota((2 * nc, SPAN), 1) < HALF
    sign = jnp.where(iota((8, FREQ), 1) % 2 == 1, -1.0, 1.0)

    def spread(slot, values):
        turned = pltpu.roll(values, HALF, 1)
        halves[2 * slot] = jnp.where(low, values, turned)
        halves[2 * slot + 1] = jnp.where(low, turned, values)

    def pick(first, second):
        return jnp.where(low, halves[first], halves[second])

    wait_bytes(a_recv, 0, nz - 1, recv_sems.at[2])
    for z in range(nz):
        spread(z, a_recv[z].reshape(2 * nc, SPAN).astype(F32))
    blocks = [pick(order[2 * i], order[2 * i + 1]).astype(BF16) for i in range(nz)]
    blocks = jnp.concatenate(blocks, axis=0)
    spec[...] = mm(jnp.concatenate([blocks, blocks], axis=1), table).reshape(
        nz, 2, nc, 2 * FREQ
    )

    groups = [slice(k, k + 8) for k in range(0, nc, 8)]

    def load(ref, *at):
        return ref[(*at, slice(0, FREQ))], ref[(*at, slice(FREQ, 2 * FREQ))]

    def store(ref, value, *at):
        ref[(*at, slice(0, FREQ))] = value[0]
        ref[(*at, slice(FREQ, 2 * FREQ))] = value[1]

    def times(total, left, right):
        (a, b), (c, d) = left, right
        re, im = a * c - b * d, a * d + b * c
        return (re, im) if total is None else (total[0] + re, total[1] + im)

    def against(total, left, right):
        (a, b), (c, d) = left, right
        re, im = a * c + b * d, a * d - b * c
        return (re, im) if total is None else (total[0] + re, total[1] + im)

    for at in groups:
        left = [load(spec, i, 0, at) for i in range(nz)]
        right = [load(spec, i, 1, at) for i in range(nz)]
        cross = []
        for d in range(nz):
            total = None
            for i in range(nz - d):
                total = against(total, left[i], right[i + d])
            cross.append(total)
        for d in range(nz):
            re, im = cross[d]
            if d + 1 < nz:
                re = re + sign * cross[d + 1][1]
                im = im - sign * cross[d + 1][0]
            store(wspec, (re, im), d, at)
    high, rest = split(wspec[...].reshape(nz * nc, 2 * FREQ))
    lags = mm_nt(high, table)
    lags = lags[:, :SPAN] + lags[:, SPAN:] + mm_nt(rest, table[:SPAN])
    g_send[...] = (lags * (1.0 / SPAN)).astype(BF16).reshape(nz, 2, nf, SPAN)

    g_slot = g_recv.at[ji]
    near = ji % 2
    for k in range(nz):
        z = first[k]
        remote(g_send.at[z, 1 - near], g_slot, 3, (z, 2 * mine + 1 - near)).start()
        if k < nz - 1:
            z = urgent[k]
            remote(g_send.at[z, near], g_slot, 3, (z, 2 * mine + near)).start()

    @pl.when(own)
    def _():
        pltpu.make_async_copy(g_send.at[zi, near], g_slot, recv_sems.at[3]).start()

    @pl.when(jnp.logical_not(own))
    def _():
        remote(g_send.at[zi, near], g_slot, 3, (zi, 2 * mine + near)).start()

    wait_bytes(f_recv, 0, nz, recv_sems.at[0])

    taps = f_recv[...].reshape(nz * nc, SPAN)
    raw = mm(jnp.concatenate([taps, taps], axis=1), table)
    wspec[...] = raw.reshape(nz, nc, 2 * FREQ)
    for at in groups:
        taps = [load(wspec, d, at) for d in range(nz)]
        for d in reversed(range(1, nz)):
            (re, im), (before_re, before_im) = taps[d], taps[d - 1]
            taps[d] = (re - sign * before_im, im + sign * before_re)
        left = [load(spec, i, 0, at) for i in range(nz)]
        for m in range(nz):
            total = None
            for i in range(m + 1):
                total = times(total, taps[m - i], left[i])
            store(sums, total, m, 0, at)
        right = [load(spec, i, 1, at) for i in range(nz)]
        for m in range(nz):
            total = None
            for j in range(m, nz):
                total = against(total, taps[j - m], right[j])
            store(sums, total, m, 1, at)
    high, rest = split(sums[...].reshape(2 * nz * nc, 2 * FREQ))
    result = mm_nt(high, table)
    result = result[:, :SPAN] + result[:, SPAN:] + mm_nt(rest, table[:SPAN])
    result = result * (1.0 / SPAN)
    for i in range(nz):
        spread(i, result[2 * nc * i : 2 * nc * (i + 1)])
    for z in range(nz):
        r_send[z] = pick(ids[2 * z], ids[2 * z + 1]).astype(BF16).reshape(2, nc, SPAN)
    for q in urgent:
        remote(r_send.at[q], r_recv.at[mine], 4, (q, ji)).start()
    r_recv[mine] = r_send[zi]

    wait_bytes(g_recv, 0, nj, recv_sems.at[3])
    total = g_recv[0].astype(F32)
    for j in range(1, nj):
        total = total + g_recv[j].astype(F32)
    fgrad_ref[...] = total

    wait_bytes(r_recv, 0, nz - 1, recv_sems.at[4])
    conv_ref[...] = r_recv[:, 0].reshape(nz * nc, SPAN)
    back_ref[...] = r_recv[:, 1].reshape(nz * nc, SPAN)

    wait_bytes(ids_all, 0, nz - 1, send_sems.at[1])
    wait_bytes(a_send, 0, nz - 1, send_sems.at[2])
    wait_bytes(r_send, 0, nz - 1, send_sems.at[4])

    @pl.when(own)
    def _():
        wait_bytes(f_recv.reshape(nj, nf, SPAN), 0, nj - 1, send_sems.at[0])
        wait_bytes(g_recv, 0, nj - 1, send_sems.at[3])

    @pl.when(jnp.logical_not(own))
    def _():
        wait_bytes(f_recv, 0, nz, send_sems.at[0])
        wait_bytes(g_recv, 0, nj, send_sems.at[3])


def gate_kernel(
    conv_ref,
    back_ref,
    fgrad_ref,
    ig_ref,
    sg_ref,
    ct_ref,
    outer_hbm,
    inner_hbm,
    signal_hbm,
    fgrad_hbm,
    outer,
    inner,
    signal,
    sems,
):
    def put(src, dst, k):
        copy = pltpu.make_async_copy(src, dst, sems.at[k])
        copy.start()
        return copy

    copies = [put(fgrad_ref, fgrad_hbm, 0)]
    conv = conv_ref[...].astype(F32).T
    outer[...] = (ct_ref[...].astype(F32) * conv).astype(BF16)
    copies.append(put(outer, outer_hbm, 1))
    back = back_ref[...].astype(F32).T
    inner[...] = (back * sg_ref[...].astype(F32)).astype(BF16)
    copies.append(put(inner, inner_hbm, 2))
    signal[...] = (back * ig_ref[...].astype(F32)).astype(BF16)
    copies.append(put(signal, signal_hbm, 3))
    for copy in copies:
        copy.wait()


def solution(mesh):
    nz = mesh.shape["ctx"]
    nj = mesh.shape["ch"]

    def local(out_gate, in_gate, signal, cotangent, filters, block_ids):
        tokens, width = out_gate.shape
        nf = filters.shape[1]
        nc = 2 * nf
        vmem = pl.BlockSpec(memory_space=pltpu.VMEM)
        anywhere = pl.BlockSpec(memory_space=pltpu.HBM)
        grad = jax.ShapeDtypeStruct((tokens, width), BF16)
        turned = jax.ShapeDtypeStruct((width, tokens), BF16)
        tokens_vmem = pltpu.VMEM((tokens, width), BF16)
        block = pltpu.VMEM((nz, 2, nc, SPAN), BF16)
        held = pl.pallas_call(
            partial(exchange_kernel, nz, nj, nf),
            out_shape=(turned, turned, jax.ShapeDtypeStruct((nf, SPAN), F32), grad, grad, grad),
            in_specs=[anywhere] * 7,
            out_specs=(vmem,) * 6,
            scratch_shapes=[
                tokens_vmem,
                pltpu.VMEM((2 * SPAN, 2 * FREQ), BF16),
                pltpu.SMEM((2,), jnp.int32),
                pltpu.SMEM((nz, 2), jnp.int32),
                pltpu.VMEM((nf, SPAN), F32),
                pltpu.VMEM((nf, SPAN), BF16),
                pltpu.VMEM((nz, 2, nf, SPAN), BF16),
                block,
                block,
                block,
                block,
                pltpu.VMEM((nz, 2, nf, SPAN), BF16),
                pltpu.VMEM((nj, nf, SPAN), BF16),
                pltpu.VMEM((2 * nz, 2 * nc, SPAN), F32),
                pltpu.VMEM((nz, 2, nc, 2 * FREQ), F32),
                pltpu.VMEM((nz, nc, 2 * FREQ), F32),
                pltpu.VMEM((nz, 2, nc, 2 * FREQ), F32),
                pltpu.SemaphoreType.DMA((7,)),
                pltpu.SemaphoreType.DMA((5,)),
                pltpu.SemaphoreType.DMA((5,)),
            ],
            compiler_params=pltpu.CompilerParams(
                collective_id=0, has_side_effects=True, vmem_limit_bytes=48 * 1024 * 1024
            ),
        )(
            *(
                pltpu.with_memory_space_constraint(value, pltpu.HBM)
                for value in (
                    block_ids,
                    out_gate,
                    in_gate,
                    signal,
                    cotangent,
                    filters.T,
                    jnp.asarray(dft_table()),
                )
            ),
        )
        *grads, fgrad = pl.pallas_call(
            gate_kernel,
            out_shape=(grad, grad, grad, jax.ShapeDtypeStruct((nf, SPAN), F32)),
            in_specs=[vmem] * 6,
            out_specs=(anywhere,) * 4,
            scratch_shapes=[tokens_vmem] * 3 + [pltpu.SemaphoreType.DMA((4,))],
            compiler_params=pltpu.CompilerParams(vmem_limit_bytes=32 * 1024 * 1024),
        )(*held)
        return (*grads, fgrad.T)

    return jax.shard_map(
        local,
        mesh=mesh,
        in_specs=(P("ctx", "ch"),) * 5 + (P("ctx"),),
        out_specs=(P("ctx", "ch"),) * 4,
        check_vma=False,
    )
```

```python
from functools import partial

import jax
import jax.numpy as jnp
import numpy as np
from jax import lax
from jax.experimental import pallas as pl
from jax.experimental.pallas import tpu as pltpu
from jax.sharding import PartitionSpec as P

MESH = pl.DeviceIdType.MESH
BF16 = jnp.bfloat16
F32 = jnp.float32
HALF = 64
SPAN = 128
FREQ = 128


def iota(shape, dim):
    return lax.broadcasted_iota(jnp.int32, shape, dim)


def dft_table():
    angle = np.pi * np.outer(np.arange(SPAN), 2 * np.arange(FREQ) + 1) / (2 * SPAN)
    full = np.concatenate([np.cos(angle), -np.sin(angle)], axis=1)
    high = full.astype(BF16)
    low = (full - high.astype(np.float64)).astype(BF16)
    return np.concatenate([high, low], axis=0)


def mm(left, right):
    return jnp.dot(left, right, preferred_element_type=F32)


def mm_nt(left, right):
    return lax.dot_general(left, right, (((1,), (1,)), ((), ())), preferred_element_type=F32)


def wait_bytes(ref, start, count, sem):
    view = ref.at[pl.ds(start, count)]
    pltpu.make_async_copy(view, view, sem).wait()


def exchange_kernel(
    nz,
    nj,
    nf,
    ids_hbm,
    og_hbm,
    ig_hbm,
    sg_hbm,
    ct_hbm,
    fl_hbm,
    dft_hbm,
    conv_ref,
    back_ref,
    fgrad_ref,
    ig_ref,
    sg_ref,
    ct_ref,
    og_ref,
    dft_ref,
    ids_ref,
    ids_all,
    fl_ref,
    f_send,
    f_recv,
    a_send,
    a_recv,
    r_send,
    r_recv,
    g_send,
    g_recv,
    halves,
    spec,
    wspec,
    load_sems,
    send_sems,
    recv_sems,
):
    nc = 2 * nf
    nx = nj // 4
    zi = lax.axis_index("ctx")
    ji = lax.axis_index("ch")
    depth, core = zi // 2, zi % 2
    xi, yi = ji // 4, ji % 4

    def chunk_of(q):
        return 2 * lax.rem(xi + q // 2 + 1, nx) + lax.rem(q + yi // 2, 2)

    def user_of(j):
        z = lax.rem(xi + 2 * nx - j // 4 - 1, nx)
        return 2 * z + lax.rem(yi // 2 + j % 4 // 2, 2)

    mine = chunk_of(zi)

    barrier = pltpu.get_barrier_semaphore()

    def greet(device):
        pl.semaphore_signal(barrier, inc=1, device_id=device, device_id_type=MESH)

    def hops(step, size):
        return min(step, size - step)

    nd = nz // 2
    steps = sorted(
        ((dz, dc) for dz in range(nd) for dc in range(2)),
        key=lambda s: (-hops(s[0], nd), -s[1]),
    )
    ctx_order = [2 * lax.rem(depth + dz, nd) + lax.rem(core + dc, 2) for dz, dc in steps]
    group = ctx_order[:-1]
    owners = [(z, 2 * mine + r) for z in ctx_order for r in range(2)]
    users = []
    for dx, dy in sorted(
        ((dx, dy) for dx in range(nx) for dy in range(4)),
        key=lambda s: -hops(s[0], nx) - hops(s[1], 4),
    ):
        j = 4 * lax.rem(xi + dx, nx) + lax.rem(yi + dy, 4)
        users.append((user_of(j), j))
    own = user_of(ji) == zi

    def gray(value):
        return value ^ (value >> 1)

    rank = 2 * gray(depth) + 1 - core
    first = [2 * gray(k // 2) + 1 - k % 2 for k in range(nz)]
    urgent = [
        jnp.where(rank <= k, first[k + 1], first[k]) for k in range(nz - 1)
    ]
    own_side = [2 * mine + r == ji for r in range(2)]

    for device in owners[:-2]:
        greet(device)
    for r in range(2):
        pl.when(jnp.logical_not(own_side[r]))(partial(greet, owners[r - 2]))
    for q in group:
        greet((q, ji))
    for step in range(1, nj):
        greet((zi, lax.rem(ji + step, nj)))

    loads = [
        pltpu.make_async_copy(src, dst, load_sems.at[k])
        for k, (src, dst) in enumerate(
            (
                (ig_hbm, ig_ref),
                (sg_hbm, sg_ref),
                (ct_hbm, ct_ref),
                (og_hbm, og_ref),
                (dft_hbm, dft_ref),
                (fl_hbm, fl_ref),
                (ids_hbm, ids_ref),
            )
        )
    ]
    for load in loads:
        load.start()

    loads[5].wait()
    f_send[...] = fl_ref[...].astype(BF16)
    loads[0].wait()
    loads[1].wait()
    product = ig_ref[...].astype(F32) * sg_ref[...].astype(F32)
    a_send[:, 0] = product.T.astype(BF16).reshape(nz, nc, SPAN)
    loads[2].wait()
    loads[3].wait()
    weighted = ct_ref[...].astype(F32) * og_ref[...].astype(F32)
    a_send[:, 1] = weighted.T.astype(BF16).reshape(nz, nc, SPAN)

    pl.semaphore_wait(barrier, nz - 2 + 2 * nj - jnp.where(own, 1, 0))

    def remote(src, dst, k, device):
        return pltpu.make_async_remote_copy(
            src, dst, send_sems.at[k], recv_sems.at[k], device, MESH
        )

    f_slot = f_recv.at[zi, yi % 2]
    loads[6].wait()
    for device in users[: nj // 4]:
        remote(f_send, f_slot, 0, device).start()
    for q in group:
        remote(ids_ref, ids_all.at[zi], 1, (q, ji)).start()
        remote(a_send.at[chunk_of(q)], a_recv.at[zi], 2, (q, ji)).start()
    for device in users[nj // 4 : -1]:
        remote(f_send, f_slot, 0, device).start()

    @pl.when(own)
    def _():
        pltpu.make_async_copy(f_send, f_slot, recv_sems.at[0]).start()

    @pl.when(jnp.logical_not(own))
    def _():
        remote(f_send, f_slot, 0, users[-1]).start()

    ids_all[zi, 0] = ids_ref[0]
    ids_all[zi, 1] = ids_ref[1]
    a_recv[zi] = a_send[mine]

    wait_bytes(ids_all, 0, nz - 1, recv_sems.at[1])
    ids = [ids_all[s // 2, s % 2] for s in range(2 * nz)]
    order = []
    for n in range(2 * nz):
        place = jnp.int32(0)
        for s in range(2 * nz):
            place = jnp.where(ids[s] == n, s, place)
        order.append(place)

    loads[4].wait()
    table = dft_ref[...]
    low = iota((2 * nc, SPAN), 1) < HALF
    sign = jnp.where(iota((8, FREQ), 1) % 2 == 1, -1.0, 1.0)

    def spread(slot, values):
        turned = pltpu.roll(values, HALF, 1)
        halves[2 * slot] = jnp.where(low, values, turned).reshape(2, nc, SPAN)
        halves[2 * slot + 1] = jnp.where(low, turned, values).reshape(2, nc, SPAN)

    def pick(first, second):
        first, second = (halves[k].reshape(2 * nc, SPAN) for k in (first, second))
        return jnp.where(low, first, second)

    wait_bytes(a_recv, 0, nz - 1, recv_sems.at[2])
    for z in range(nz):
        spread(z, a_recv[z].reshape(2 * nc, SPAN).astype(F32))
    blocks = [pick(order[2 * i], order[2 * i + 1]).astype(BF16) for i in range(nz)]
    blocks = jnp.concatenate(blocks, axis=0)
    spec[...] = mm(jnp.concatenate([blocks, blocks], axis=1), table).reshape(
        nz, 2, nc, 2 * FREQ
    )

    groups = [slice(k, k + 8) for k in range(0, nc, 8)]

    def load(ref, *at):
        return ref[(*at, slice(0, FREQ))], ref[(*at, slice(FREQ, 2 * FREQ))]

    def inverse(parts):
        rows = jnp.concatenate([jnp.concatenate(part, axis=1) for part in parts], axis=0)
        points = mm_nt(rows.astype(BF16), table)
        return (points[:, :SPAN] + points[:, SPAN:]) * (1.0 / SPAN)

    def times(total, left, right):
        (a, b), (c, d) = left, right
        re, im = a * c - b * d, a * d + b * c
        return (re, im) if total is None else (total[0] + re, total[1] + im)

    def against(total, left, right):
        (a, b), (c, d) = left, right
        re, im = a * c + b * d, a * d - b * c
        return (re, im) if total is None else (total[0] + re, total[1] + im)

    for r in range(2):
        parts = [[None, None] for _ in range(nz)]
        for k in range(2):
            at = groups[2 * r + k]
            left = [load(spec, i, 0, at) for i in range(nz)]
            right = [load(spec, i, 1, at) for i in range(nz)]
            cross = []
            for d in range(nz):
                total = None
                for i in range(nz - d):
                    total = against(total, left[i], right[i + d])
                cross.append(total)
            for d in range(nz):
                re, im = cross[d]
                if d + 1 < nz:
                    re = re + sign * cross[d + 1][1]
                    im = im - sign * cross[d + 1][0]
                parts[d][k] = (re, im)
        lags = inverse([part for pair in parts for part in pair])
        g_send[:, r] = lags.astype(BF16).reshape(nz, nf, SPAN)

    g_slot = g_recv.at[ji]
    near = ji % 2
    for k in range(nz):
        z = first[k]
        remote(g_send.at[z, 1 - near], g_slot, 3, (z, 2 * mine + 1 - near)).start()
        if k < nz - 1:
            z = urgent[k]
            remote(g_send.at[z, near], g_slot, 3, (z, 2 * mine + near)).start()

    @pl.when(own)
    def _():
        pltpu.make_async_copy(g_send.at[zi, near], g_slot, recv_sems.at[3]).start()

    @pl.when(jnp.logical_not(own))
    def _():
        remote(g_send.at[zi, near], g_slot, 3, (zi, 2 * mine + near)).start()

    wait_bytes(f_recv, 0, nz, recv_sems.at[0])

    taps = f_recv[...].reshape(nz * nc, SPAN)
    raw = mm(jnp.concatenate([taps, taps], axis=1), table)
    wspec[...] = raw.reshape(nz, nc, 2 * FREQ)
    for at in groups:
        taps = [load(wspec, d, at) for d in range(nz)]
        for d in reversed(range(1, nz)):
            (re, im), (before_re, before_im) = taps[d], taps[d - 1]
            taps[d] = (re - sign * before_im, im + sign * before_re)
        parts = []
        left = [load(spec, i, 0, at) for i in range(nz)]
        for m in range(nz):
            total = None
            for i in range(m + 1):
                total = times(total, taps[m - i], left[i])
            parts.append(total)
        right = [load(spec, i, 1, at) for i in range(nz)]
        for m in range(nz):
            total = None
            for j in range(m, nz):
                total = against(total, taps[j - m], right[j])
            parts.append(total)
        points = inverse(parts)
        low8 = iota((8, SPAN), 1) < HALF
        for i in range(nz):
            for kind in range(2):
                row = 8 * (kind * nz + i)
                block = points[row : row + 8]
                turned = pltpu.roll(block, HALF, 1)
                halves[2 * i, kind, at] = jnp.where(low8, block, turned)
                halves[2 * i + 1, kind, at] = jnp.where(low8, turned, block)
    for z in range(nz):
        r_send[z] = pick(ids[2 * z], ids[2 * z + 1]).astype(BF16).reshape(2, nc, SPAN)
    for q in urgent:
        remote(r_send.at[q], r_recv.at[mine], 4, (q, ji)).start()
    r_recv[mine] = r_send[zi]

    wait_bytes(g_recv, 0, nj, recv_sems.at[3])
    total = g_recv[0].astype(F32)
    for j in range(1, nj):
        total = total + g_recv[j].astype(F32)
    fgrad_ref[...] = total

    wait_bytes(r_recv, 0, nz - 1, recv_sems.at[4])
    conv_ref[...] = r_recv[:, 0].reshape(nz * nc, SPAN)
    back_ref[...] = r_recv[:, 1].reshape(nz * nc, SPAN)

    wait_bytes(ids_all, 0, nz - 1, send_sems.at[1])
    wait_bytes(a_send, 0, nz - 1, send_sems.at[2])
    wait_bytes(r_send, 0, nz - 1, send_sems.at[4])

    @pl.when(own)
    def _():
        wait_bytes(f_recv.reshape(nj, nf, SPAN), 0, nj - 1, send_sems.at[0])
        wait_bytes(g_recv, 0, nj - 1, send_sems.at[3])

    @pl.when(jnp.logical_not(own))
    def _():
        wait_bytes(f_recv, 0, nz, send_sems.at[0])
        wait_bytes(g_recv, 0, nj, send_sems.at[3])


def gate_kernel(
    conv_ref,
    back_ref,
    fgrad_ref,
    ig_ref,
    sg_ref,
    ct_ref,
    outer_hbm,
    inner_hbm,
    signal_hbm,
    fgrad_hbm,
    outer,
    inner,
    signal,
    sems,
):
    def put(src, dst, k):
        copy = pltpu.make_async_copy(src, dst, sems.at[k])
        copy.start()
        return copy

    copies = [put(fgrad_ref, fgrad_hbm, 0)]
    conv = conv_ref[...].astype(F32).T
    outer[...] = (ct_ref[...].astype(F32) * conv).astype(BF16)
    copies.append(put(outer, outer_hbm, 1))
    back = back_ref[...].astype(F32).T
    inner[...] = (back * sg_ref[...].astype(F32)).astype(BF16)
    copies.append(put(inner, inner_hbm, 2))
    signal[...] = (back * ig_ref[...].astype(F32)).astype(BF16)
    copies.append(put(signal, signal_hbm, 3))
    for copy in copies:
        copy.wait()


def solution(mesh):
    nz = mesh.shape["ctx"]
    nj = mesh.shape["ch"]

    def local(out_gate, in_gate, signal, cotangent, filters, block_ids):
        tokens, width = out_gate.shape
        nf = filters.shape[1]
        nc = 2 * nf
        vmem = pl.BlockSpec(memory_space=pltpu.VMEM)
        anywhere = pl.BlockSpec(memory_space=pltpu.HBM)
        grad = jax.ShapeDtypeStruct((tokens, width), BF16)
        turned = jax.ShapeDtypeStruct((width, tokens), BF16)
        tokens_vmem = pltpu.VMEM((tokens, width), BF16)
        block = pltpu.VMEM((nz, 2, nc, SPAN), BF16)
        held = pl.pallas_call(
            partial(exchange_kernel, nz, nj, nf),
            out_shape=(turned, turned, jax.ShapeDtypeStruct((nf, SPAN), F32), grad, grad, grad),
            in_specs=[anywhere] * 7,
            out_specs=(vmem,) * 6,
            scratch_shapes=[
                tokens_vmem,
                pltpu.VMEM((2 * SPAN, 2 * FREQ), BF16),
                pltpu.SMEM((2,), jnp.int32),
                pltpu.SMEM((nz, 2), jnp.int32),
                pltpu.VMEM((nf, SPAN), F32),
                pltpu.VMEM((nf, SPAN), BF16),
                pltpu.VMEM((nz, 2, nf, SPAN), BF16),
                block,
                block,
                block,
                block,
                pltpu.VMEM((nz, 2, nf, SPAN), BF16),
                pltpu.VMEM((nj, nf, SPAN), BF16),
                pltpu.VMEM((2 * nz, 2, nc, SPAN), F32),
                pltpu.VMEM((nz, 2, nc, 2 * FREQ), F32),
                pltpu.VMEM((nz, nc, 2 * FREQ), F32),
                pltpu.SemaphoreType.DMA((7,)),
                pltpu.SemaphoreType.DMA((5,)),
                pltpu.SemaphoreType.DMA((5,)),
            ],
            compiler_params=pltpu.CompilerParams(
                collective_id=0, has_side_effects=True, vmem_limit_bytes=48 * 1024 * 1024
            ),
        )(
            *(
                pltpu.with_memory_space_constraint(value, pltpu.HBM)
                for value in (
                    block_ids,
                    out_gate,
                    in_gate,
                    signal,
                    cotangent,
                    filters.T,
                    jnp.asarray(dft_table()),
                )
            ),
        )
        *grads, fgrad = pl.pallas_call(
            gate_kernel,
            out_shape=(grad, grad, grad, jax.ShapeDtypeStruct((nf, SPAN), F32)),
            in_specs=[vmem] * 6,
            out_specs=(anywhere,) * 4,
            scratch_shapes=[tokens_vmem] * 3 + [pltpu.SemaphoreType.DMA((4,))],
            compiler_params=pltpu.CompilerParams(vmem_limit_bytes=32 * 1024 * 1024),
        )(*held)
        return (*grads, fgrad.T)

    return jax.shard_map(
        local,
        mesh=mesh,
        in_specs=(P("ctx", "ch"),) * 5 + (P("ctx"),),
        out_specs=(P("ctx", "ch"),) * 4,
        check_vma=False,
    )
```

```python
from functools import partial

import jax
import jax.numpy as jnp
import numpy as np
from jax import lax
from jax.experimental import pallas as pl
from jax.experimental.pallas import tpu as pltpu
from jax.sharding import PartitionSpec as P

MESH = pl.DeviceIdType.MESH
BF16 = jnp.bfloat16
F32 = jnp.float32
HALF = 64
SPAN = 128
FREQ = 128


def iota(shape, dim):
    return lax.broadcasted_iota(jnp.int32, shape, dim)


def dft_table():
    angle = np.pi * np.outer(np.arange(SPAN), 2 * np.arange(FREQ) + 1) / (2 * SPAN)
    full = np.concatenate([np.cos(angle), -np.sin(angle)], axis=1)
    high = full.astype(BF16)
    low = (full - high.astype(np.float64)).astype(BF16)
    return np.concatenate([high, low], axis=0)


def mm(left, right):
    return jnp.dot(left, right, preferred_element_type=F32)


def mm_nt(left, right):
    return lax.dot_general(left, right, (((1,), (1,)), ((), ())), preferred_element_type=F32)


def wait_bytes(ref, start, count, sem):
    view = ref.at[pl.ds(start, count)]
    pltpu.make_async_copy(view, view, sem).wait()


def exchange_kernel(
    nz,
    nj,
    nf,
    ids_hbm,
    og_hbm,
    ig_hbm,
    sg_hbm,
    ct_hbm,
    fl_hbm,
    dft_hbm,
    conv_ref,
    back_ref,
    fgrad_ref,
    ig_ref,
    sg_ref,
    ct_ref,
    og_ref,
    dft_ref,
    ids_ref,
    ids_all,
    fl_ref,
    f_send,
    f_recv,
    a_send,
    a_recv,
    r_send,
    r_recv,
    g_send,
    g_recv,
    halves,
    spec,
    wspec,
    load_sems,
    send_sems,
    recv_sems,
):
    nc = 2 * nf
    nx = nj // 4
    zi = lax.axis_index("ctx")
    ji = lax.axis_index("ch")
    depth, core = zi // 2, zi % 2
    xi, yi = ji // 4, ji % 4

    def chunk_of(q):
        return 2 * lax.rem(xi + q // 2 + 1, nx) + lax.rem(q + yi // 2, 2)

    def user_of(j):
        z = lax.rem(xi + 2 * nx - j // 4 - 1, nx)
        return 2 * z + lax.rem(yi // 2 + j % 4 // 2, 2)

    mine = chunk_of(zi)

    barrier = pltpu.get_barrier_semaphore()

    def greet(device):
        pl.semaphore_signal(barrier, inc=1, device_id=device, device_id_type=MESH)

    def hops(step, size):
        return min(step, size - step)

    nd = nz // 2
    steps = sorted(
        ((dz, dc) for dz in range(nd) for dc in range(2)),
        key=lambda s: (-hops(s[0], nd), -s[1]),
    )
    ctx_order = [2 * lax.rem(depth + dz, nd) + lax.rem(core + dc, 2) for dz, dc in steps]
    group = ctx_order[:-1]
    owners = [(z, 2 * mine + r) for z in ctx_order for r in range(2)]
    users = []
    for dx, dy in sorted(
        ((dx, dy) for dx in range(nx) for dy in range(4)),
        key=lambda s: -hops(s[0], nx) - hops(s[1], 4),
    ):
        j = 4 * lax.rem(xi + dx, nx) + lax.rem(yi + dy, 4)
        users.append((user_of(j), j))
    own = user_of(ji) == zi

    def gray(value):
        return value ^ (value >> 1)

    rank = 2 * gray(depth) + 1 - core
    first = [2 * gray(k // 2) + 1 - k % 2 for k in range(nz)]
    urgent = [
        jnp.where(rank <= k, first[k + 1], first[k]) for k in range(nz - 1)
    ]
    own_side = [2 * mine + r == ji for r in range(2)]

    for device in owners[:-2]:
        greet(device)
    for r in range(2):
        pl.when(jnp.logical_not(own_side[r]))(partial(greet, owners[r - 2]))
    for q in group:
        greet((q, ji))
    for step in range(1, nj):
        greet((zi, lax.rem(ji + step, nj)))

    loads = [
        pltpu.make_async_copy(src, dst, load_sems.at[k])
        for k, (src, dst) in enumerate(
            (
                (ig_hbm, ig_ref),
                (sg_hbm, sg_ref),
                (ct_hbm, ct_ref),
                (og_hbm, og_ref),
                (dft_hbm, dft_ref),
                (fl_hbm, fl_ref),
                (ids_hbm, ids_ref),
            )
        )
    ]
    for load in loads:
        load.start()

    loads[5].wait()
    f_send[...] = fl_ref[...].astype(BF16)
    loads[0].wait()
    loads[1].wait()
    product = ig_ref[...].astype(F32) * sg_ref[...].astype(F32)
    a_send[:, 0] = product.T.astype(BF16).reshape(nz, nc, SPAN)
    loads[2].wait()
    loads[3].wait()
    weighted = ct_ref[...].astype(F32) * og_ref[...].astype(F32)
    a_send[:, 1] = weighted.T.astype(BF16).reshape(nz, nc, SPAN)

    pl.semaphore_wait(barrier, nz - 2 + 2 * nj - jnp.where(own, 1, 0))

    def remote(src, dst, k, device):
        return pltpu.make_async_remote_copy(
            src, dst, send_sems.at[k], recv_sems.at[k], device, MESH
        )

    loads[6].wait()
    for q in group:
        remote(ids_ref, ids_all.at[zi], 1, (q, ji)).start()
    ids_all[zi, 0] = ids_ref[0]
    ids_all[zi, 1] = ids_ref[1]

    f_slot = f_recv.at[zi, yi % 2]
    for device in users[: nj // 4]:
        remote(f_send, f_slot, 0, device).start()
    for q in group:
        remote(a_send.at[chunk_of(q)], a_recv.at[zi], 2, (q, ji)).start()
    for device in users[nj // 4 : -1]:
        remote(f_send, f_slot, 0, device).start()

    @pl.when(own)
    def _():
        pltpu.make_async_copy(f_send, f_slot, recv_sems.at[0]).start()

    @pl.when(jnp.logical_not(own))
    def _():
        remote(f_send, f_slot, 0, users[-1]).start()

    a_recv[zi] = a_send[mine]

    wait_bytes(ids_all, 0, nz - 1, recv_sems.at[1])
    ids = [ids_all[s // 2, s % 2] for s in range(2 * nz)]
    low_word = high_word = jnp.int32(0)
    for s in range(1, 2 * nz):
        place = s << (4 * (ids[s] & 7))
        low_word = low_word + jnp.where(ids[s] < 8, place, 0)
        high_word = high_word + jnp.where(ids[s] < 8, 0, place)
    order = [
        lax.shift_right_logical(low_word if n < 8 else high_word, jnp.int32(4 * (n % 8))) & 15
        for n in range(2 * nz)
    ]

    loads[4].wait()
    table = dft_ref[...]
    low = iota((2 * nc, SPAN), 1) < HALF
    sign = jnp.where(iota((8, FREQ), 1) % 2 == 1, -1.0, 1.0)

    def spread(slot, values):
        turned = pltpu.roll(values, HALF, 1)
        halves[2 * slot] = jnp.where(low, values, turned).reshape(2, nc, SPAN)
        halves[2 * slot + 1] = jnp.where(low, turned, values).reshape(2, nc, SPAN)

    def pick(first, second):
        first, second = (halves[k].reshape(2 * nc, SPAN) for k in (first, second))
        return jnp.where(low, first, second)

    wait_bytes(a_recv, 0, nz - 1, recv_sems.at[2])
    for z in range(nz):
        spread(z, a_recv[z].reshape(2 * nc, SPAN).astype(F32))
    blocks = [pick(order[2 * i], order[2 * i + 1]).astype(BF16) for i in range(nz)]
    blocks = jnp.concatenate(blocks, axis=0)
    spec[...] = mm(jnp.concatenate([blocks, blocks], axis=1), table).reshape(
        nz, 2, nc, 2 * FREQ
    )

    groups = [slice(k, k + 8) for k in range(0, nc, 8)]

    def load(ref, *at):
        return ref[(*at, slice(0, FREQ))], ref[(*at, slice(FREQ, 2 * FREQ))]

    def inverse(parts):
        rows = jnp.concatenate([jnp.concatenate(part, axis=1) for part in parts], axis=0)
        points = mm_nt(rows.astype(BF16), table)
        return (points[:, :SPAN] + points[:, SPAN:]) * (1.0 / SPAN)

    def times(total, left, right):
        (a, b), (c, d) = left, right
        re, im = a * c - b * d, a * d + b * c
        return (re, im) if total is None else (total[0] + re, total[1] + im)

    def against(total, left, right):
        (a, b), (c, d) = left, right
        re, im = a * c + b * d, a * d - b * c
        return (re, im) if total is None else (total[0] + re, total[1] + im)

    for r in range(2):
        parts = [[None, None] for _ in range(nz)]
        for k in range(2):
            at = groups[2 * r + k]
            left = [load(spec, i, 0, at) for i in range(nz)]
            right = [load(spec, i, 1, at) for i in range(nz)]
            cross = []
            for d in range(nz):
                total = None
                for i in range(nz - d):
                    total = against(total, left[i], right[i + d])
                cross.append(total)
            for d in range(nz):
                re, im = cross[d]
                if d + 1 < nz:
                    re = re + sign * cross[d + 1][1]
                    im = im - sign * cross[d + 1][0]
                parts[d][k] = (re, im)
        lags = inverse([part for pair in parts for part in pair])
        g_send[:, r] = lags.astype(BF16).reshape(nz, nf, SPAN)

    g_slot = g_recv.at[ji]
    near = ji % 2
    for k in range(nz):
        z = first[k]
        remote(g_send.at[z, 1 - near], g_slot, 3, (z, 2 * mine + 1 - near)).start()
        if k < nz - 1:
            z = urgent[k]
            remote(g_send.at[z, near], g_slot, 3, (z, 2 * mine + near)).start()

    @pl.when(own)
    def _():
        pltpu.make_async_copy(g_send.at[zi, near], g_slot, recv_sems.at[3]).start()

    @pl.when(jnp.logical_not(own))
    def _():
        remote(g_send.at[zi, near], g_slot, 3, (zi, 2 * mine + near)).start()

    wait_bytes(f_recv, 0, nz, recv_sems.at[0])

    taps = f_recv[...].reshape(nz * nc, SPAN)
    raw = mm(jnp.concatenate([taps, taps], axis=1), table)
    wspec[...] = raw.reshape(nz, nc, 2 * FREQ)
    for at in groups:
        taps = [load(wspec, d, at) for d in range(nz)]
        for d in reversed(range(1, nz)):
            (re, im), (before_re, before_im) = taps[d], taps[d - 1]
            taps[d] = (re - sign * before_im, im + sign * before_re)
        parts = []
        left = [load(spec, i, 0, at) for i in range(nz)]
        for m in range(nz):
            total = None
            for i in range(m + 1):
                total = times(total, taps[m - i], left[i])
            parts.append(total)
        right = [load(spec, i, 1, at) for i in range(nz)]
        for m in range(nz):
            total = None
            for j in range(m, nz):
                total = against(total, taps[j - m], right[j])
            parts.append(total)
        points = inverse(parts)
        low8 = iota((8, SPAN), 1) < HALF
        for i in range(nz):
            for kind in range(2):
                row = 8 * (kind * nz + i)
                block = points[row : row + 8]
                turned = pltpu.roll(block, HALF, 1)
                halves[2 * i, kind, at] = jnp.where(low8, block, turned)
                halves[2 * i + 1, kind, at] = jnp.where(low8, turned, block)
    for z in range(nz):
        r_send[z] = pick(ids[2 * z], ids[2 * z + 1]).astype(BF16).reshape(2, nc, SPAN)
    for q in urgent:
        remote(r_send.at[q], r_recv.at[mine], 4, (q, ji)).start()
    r_recv[mine] = r_send[zi]

    wait_bytes(g_recv, 0, nj, recv_sems.at[3])
    total = g_recv[0].astype(F32)
    for j in range(1, nj):
        total = total + g_recv[j].astype(F32)
    fgrad_ref[...] = total

    wait_bytes(r_recv, 0, nz - 1, recv_sems.at[4])
    conv_ref[...] = r_recv[:, 0].reshape(nz * nc, SPAN)
    back_ref[...] = r_recv[:, 1].reshape(nz * nc, SPAN)

    wait_bytes(ids_all, 0, nz - 1, send_sems.at[1])
    wait_bytes(a_send, 0, nz - 1, send_sems.at[2])
    wait_bytes(r_send, 0, nz - 1, send_sems.at[4])

    @pl.when(own)
    def _():
        wait_bytes(f_recv.reshape(nj, nf, SPAN), 0, nj - 1, send_sems.at[0])
        wait_bytes(g_recv, 0, nj - 1, send_sems.at[3])

    @pl.when(jnp.logical_not(own))
    def _():
        wait_bytes(f_recv, 0, nz, send_sems.at[0])
        wait_bytes(g_recv, 0, nj, send_sems.at[3])


def gate_kernel(
    conv_ref,
    back_ref,
    fgrad_ref,
    ig_ref,
    sg_ref,
    ct_ref,
    outer_hbm,
    inner_hbm,
    signal_hbm,
    fgrad_hbm,
    outer,
    inner,
    signal,
    sems,
):
    def put(src, dst, k):
        copy = pltpu.make_async_copy(src, dst, sems.at[k])
        copy.start()
        return copy

    copies = [put(fgrad_ref, fgrad_hbm, 0)]
    conv = conv_ref[...].astype(F32).T
    outer[...] = (ct_ref[...].astype(F32) * conv).astype(BF16)
    copies.append(put(outer, outer_hbm, 1))
    back = back_ref[...].astype(F32).T
    inner[...] = (back * sg_ref[...].astype(F32)).astype(BF16)
    copies.append(put(inner, inner_hbm, 2))
    signal[...] = (back * ig_ref[...].astype(F32)).astype(BF16)
    copies.append(put(signal, signal_hbm, 3))
    for copy in copies:
        copy.wait()


def solution(mesh):
    nz = mesh.shape["ctx"]
    nj = mesh.shape["ch"]

    def local(out_gate, in_gate, signal, cotangent, filters, block_ids):
        tokens, width = out_gate.shape
        nf = filters.shape[1]
        nc = 2 * nf
        vmem = pl.BlockSpec(memory_space=pltpu.VMEM)
        anywhere = pl.BlockSpec(memory_space=pltpu.HBM)
        grad = jax.ShapeDtypeStruct((tokens, width), BF16)
        turned = jax.ShapeDtypeStruct((width, tokens), BF16)
        tokens_vmem = pltpu.VMEM((tokens, width), BF16)
        block = pltpu.VMEM((nz, 2, nc, SPAN), BF16)
        held = pl.pallas_call(
            partial(exchange_kernel, nz, nj, nf),
            out_shape=(turned, turned, jax.ShapeDtypeStruct((nf, SPAN), F32), grad, grad, grad),
            in_specs=[anywhere] * 7,
            out_specs=(vmem,) * 6,
            scratch_shapes=[
                tokens_vmem,
                pltpu.VMEM((2 * SPAN, 2 * FREQ), BF16),
                pltpu.SMEM((2,), jnp.int32),
                pltpu.SMEM((nz, 2), jnp.int32),
                pltpu.VMEM((nf, SPAN), F32),
                pltpu.VMEM((nf, SPAN), BF16),
                pltpu.VMEM((nz, 2, nf, SPAN), BF16),
                block,
                block,
                block,
                block,
                pltpu.VMEM((nz, 2, nf, SPAN), BF16),
                pltpu.VMEM((nj, nf, SPAN), BF16),
                pltpu.VMEM((2 * nz, 2, nc, SPAN), F32),
                pltpu.VMEM((nz, 2, nc, 2 * FREQ), F32),
                pltpu.VMEM((nz, nc, 2 * FREQ), F32),
                pltpu.SemaphoreType.DMA((7,)),
                pltpu.SemaphoreType.DMA((5,)),
                pltpu.SemaphoreType.DMA((5,)),
            ],
            compiler_params=pltpu.CompilerParams(
                collective_id=0, has_side_effects=True, vmem_limit_bytes=48 * 1024 * 1024
            ),
        )(
            *(
                pltpu.with_memory_space_constraint(value, pltpu.HBM)
                for value in (
                    block_ids,
                    out_gate,
                    in_gate,
                    signal,
                    cotangent,
                    filters.T,
                    jnp.asarray(dft_table()),
                )
            ),
        )
        *grads, fgrad = pl.pallas_call(
            gate_kernel,
            out_shape=(grad, grad, grad, jax.ShapeDtypeStruct((nf, SPAN), F32)),
            in_specs=[vmem] * 6,
            out_specs=(anywhere,) * 4,
            scratch_shapes=[tokens_vmem] * 3 + [pltpu.SemaphoreType.DMA((4,))],
            compiler_params=pltpu.CompilerParams(vmem_limit_bytes=32 * 1024 * 1024),
        )(*held)
        return (*grads, fgrad.T)

    return jax.shard_map(
        local,
        mesh=mesh,
        in_specs=(P("ctx", "ch"),) * 5 + (P("ctx"),),
        out_specs=(P("ctx", "ch"),) * 4,
        check_vma=False,
    )
```
